256 devices in a mesh: pool: 32 (over y, x, core), head: 8 (over z).
Axes of the slice: x: 4, y: 4, z: 8, core: 2. Of those that a mesh axis runs over, the one named last changes fastest.
Arguments:
- pool_rows: bfloat16 [65536, 8192], P('pool', 'head')
- hit_owner: int32 [512], replicated, may hold values from 0 to 511, as said below
- norm_gain: float32 [8192], P('head'), may hold values from 0.1 to 1.9
- kv_weight: bfloat16 [8192, 2048], P('head'), may hold values from -0.0625 to 0.0625
- queries: bfloat16 [256, 8192], P('pool', 'head')
- row_prefix: int32 [256], replicated, may hold values from 0 to 127
- row_length: int32 [256], P('pool'), may hold values from 2 to 512, as said below
- block_table: int32 [256, 4], P('pool'), may hold values from 0 to 31, as said below
- cache_keys: bfloat16 [8, 1024, 128, 128], P('head', 'pool')
- cache_values: bfloat16 [8, 1024, 128, 128], P('head', 'pool'), may hold values from -6 to 6
Outputs:
- prefix_cache: bfloat16 [8, 256, 65536], P('head', None, 'pool')
- attended: bfloat16 [256, 8192], P('pool', 'head')
The draws below stay inside these ranges and needn't reach their ends.
Inputs may be any that keep to these rules, and one draw needn't show every extreme that they name: Every pool block is named exactly once. The 16 hit blocks k of one recompute group (the same floor(k / 16)) lie on distinct pool indices (floor(hit_owner / 16)), and the blocks of one pool index go to distinct groups. `row_length`: some row has exactly 512 resident tokens. `block_table`: the rows of one pool index name each of its 32 pages exactly once.
All inputs are finite; a program needn't handle non-finite values.
Results may differ from the reference program's by a relative error of at most 0.035.
Values may be sent and summed in bfloat16 or wider, within the bound.
A program may use at most 128 MiB of HBM per device.

```python
import math
import jax
import jax.numpy as jnp
from jax import lax

D = 8192
HEAD_DIM = 128
QUERY_GROUP = 8
BLOCK = 128
PIECES = 4
GROUP_BLOCKS = 16
ROWS_DEV = 8
ROW_BLOCKS = 4
KV_HEADS = 8
Q_HEADS = 64
HITS = 512
PREFIXES = 128
ROWS = 256
CONTEXT = 512
N_HEAD = 8


def shared_rows(key):
    table_key = jax.random.fold_in(key, 0)
    owners = ROWS // ROWS_DEV
    pages = ROWS_DEV * ROW_BLOCKS
    tables = jax.vmap(lambda single: jax.random.permutation(single, pages))(jax.random.split(table_key, owners))
    table = tables.reshape(ROWS, ROW_BLOCKS).astype(jnp.int32)
    return table


def key_field(key):
    key = jax.random.fold_in(key, 11)
    normal_key = jax.random.fold_in(key, 0)
    shape = (KV_HEADS, ROWS * ROW_BLOCKS, BLOCK, HEAD_DIM)
    normal_part = jax.random.normal(normal_key, shape, dtype=jnp.float32)
    return normal_part


def draw_block_table(key, part):
    table = shared_rows(key)
    return table


def draw_cache_keys(key, part):
    field = key_field(key)
    return field.astype(jnp.bfloat16)


def draw_queries(key, part):
    own_key = jax.random.fold_in(key, 13)
    return jax.random.normal(own_key, (ROWS, Q_HEADS * HEAD_DIM), dtype=jnp.float32).astype(jnp.bfloat16)


def draw_pool_rows(key, part):
    key = jax.random.fold_in(key, 5)
    entry_key, scale_key = jax.random.split(key)
    shape = (HITS * BLOCK, D)
    column = jnp.arange(D, dtype=jnp.float32) / D
    entries = jax.random.normal(entry_key, shape, dtype=jnp.float32)
    rising = 3.0 ** column
    row_scale = jnp.exp(jax.random.uniform(scale_key, (HITS * BLOCK, 1), jnp.float32, math.log(0.3), math.log(3.0)))
    return (entries * rising[None, :] * row_scale).astype(jnp.bfloat16)


def draw_row_length(key, part):
    key = jax.random.fold_in(key, 7)
    length_key, place_key = jax.random.split(key)
    lengths = jax.random.randint(length_key, (ROWS,), 2, CONTEXT + 1)
    place = jax.random.randint(place_key, (), 0, ROWS)
    return lengths.at[place].set(CONTEXT).astype(jnp.int32)


def draw_hit_owner(key, part):
    key = jax.random.fold_in(key, 9)
    owners = HITS // GROUP_BLOCKS
    keys = jax.random.split(key, 5)
    sigma = jax.random.permutation(keys[0], owners)
    tau = jax.random.permutation(keys[1], owners)
    offsets = jax.random.permutation(keys[2], owners)[:GROUP_BLOCKS]
    turn = jax.random.randint(keys[3], (owners,), 0, GROUP_BLOCKS)
    slot_perm = jax.vmap(lambda single: jax.random.permutation(single, GROUP_BLOCKS))(jax.random.split(keys[4], owners))
    owner_ids = jnp.arange(owners, dtype=jnp.int32)[:, None]
    logical = jnp.arange(GROUP_BLOCKS, dtype=jnp.int32)[None, :]
    groups = tau[(sigma[owner_ids] + offsets[logical]) % owners]
    places = (logical + turn[groups]) % GROUP_BLOCKS
    values = owner_ids * GROUP_BLOCKS + slot_perm
    result = jnp.zeros((HITS,), jnp.int32)
    return result.at[(groups * GROUP_BLOCKS + places).reshape(-1)].set(values.reshape(-1).astype(jnp.int32))


def with_ends(values, stream_key, least, top_value):
    spot = [jax.random.randint(jax.random.fold_in(stream_key, axis), (), 0, length) for axis, length in enumerate(values.shape)]
    widest = values.shape.index(max(values.shape))
    next_to = spot[:widest] + [(spot[widest] + 1) % values.shape[widest]] + spot[widest + 1:]
    return values.at[tuple(spot)].set(least).at[tuple(next_to)].set(top_value)


def block_levels(stream_key, shape, pieces, least, top_value):
    level, own = 1.0, jax.random.fold_in(stream_key, 6)
    for dim, blocks in pieces:
        heights = jnp.exp(jax.random.uniform(jax.random.fold_in(own, dim), (blocks,), jnp.float32, least / len(pieces), top_value / len(pieces)))
        level = level * jnp.repeat(heights, shape[dim] // blocks).reshape([-1 if axis == dim else 1 for axis in range(len(shape))])
    return level


def normal_values(stream_key, extent, scale, most, pieces=(), kind=jnp.bfloat16):
    values = jax.random.normal(stream_key, extent, jnp.float32) * scale
    if len(pieces) > 0:
        values = block_levels(stream_key, extent, pieces, -0.22, 0.18) * values
    return jnp.clip(values, min=-most, max=most).astype(kind)


def setup_inputs(seed: int = 0) -> dict:
    seeds = jax.random.split(jax.random.key(seed), 11)
    pool_rows = draw_pool_rows(jax.random.fold_in(seeds[10], 71), 0)
    hit_owner = draw_hit_owner(jax.random.fold_in(seeds[10], 71), 0)
    norm_gain = jnp.clip(1.0 + 0.18 * jax.random.normal(seeds[2], (D,), jnp.float32), 0.1, 1.9)
    kv_weight = normal_values(seeds[3], (D, 2 * HEAD_DIM * KV_HEADS), D ** -0.5, 0.0625, ((0, 8),))
    queries = draw_queries(jax.random.fold_in(seeds[10], 71), 0)
    row_prefix = with_ends(jax.random.randint(seeds[5], (ROWS,), 0, PREFIXES), jax.random.fold_in(seeds[5], 1), 0, PREFIXES - 1).astype(jnp.int32)
    row_length = draw_row_length(jax.random.fold_in(seeds[10], 71), 0)
    block_table = draw_block_table(jax.random.fold_in(seeds[10], 71), 0)
    cache_keys = draw_cache_keys(jax.random.fold_in(seeds[10], 71), 0)
    cache_values = normal_values(seeds[9], (KV_HEADS, ROWS * ROW_BLOCKS, BLOCK, HEAD_DIM), 1.0, 6.0, ((0, 8), (1, 32)))
    return {"pool_rows": pool_rows, "hit_owner": hit_owner, "norm_gain": norm_gain, "kv_weight": kv_weight, "queries": queries, "row_prefix": row_prefix, "row_length": row_length, "block_table": block_table, "cache_keys": cache_keys, "cache_values": cache_values}


def rotate_keys(keys, positions):
    half = keys.shape[1] // 2
    frequency_index = jnp.arange(half, dtype=jnp.float32)
    freqs = jnp.exp(frequency_index * (-2.0 / keys.shape[1]) * math.log(500000.0))
    angles = positions.astype(jnp.float32)[None, :] * freqs[:, None]
    cosine = jnp.cos(angles)[None]
    sine = jnp.sin(angles)[None]
    first = keys[:, :half]
    second = keys[:, half:]
    return jnp.concatenate([first * cosine - second * sine, second * cosine + first * sine], axis=1)

def reference(pool_rows, hit_owner, norm_gain, kv_weight, queries, row_prefix, row_length, block_table, cache_keys, cache_values):
    highest = lax.Precision.HIGHEST
    slice_width = D // N_HEAD
    blocks = pool_rows.reshape(HITS, BLOCK, D)
    weight_slices = kv_weight.astype(jnp.float32).reshape(N_HEAD, slice_width, 2 * HEAD_DIM * KV_HEADS)
    gain = norm_gain.astype(jnp.float32)
    offsets = jnp.arange(BLOCK, dtype=jnp.int32)

    def recompute(hit):
        token_rows = lax.dynamic_index_in_dim(blocks, hit_owner[hit], 0, keepdims=False).astype(jnp.float32)
        inverse = lax.rsqrt(lax.optimization_barrier(jnp.mean(token_rows * token_rows, axis=1)) + 1e-05)
        scaled = (token_rows * gain[None, :]).astype(jnp.bfloat16)
        scaled = lax.optimization_barrier(scaled).astype(jnp.float32).reshape(BLOCK, N_HEAD, slice_width)
        parts = jnp.einsum('thd,hdc->htc', scaled, weight_slices, precision=highest).astype(jnp.bfloat16)
        parts = lax.optimization_barrier(parts).astype(jnp.float32)
        projected = (lax.optimization_barrier(jnp.sum(parts, axis=0)) * inverse[:, None]).T.reshape(KV_HEADS, 2 * HEAD_DIM, BLOCK)
        positions = hit % PIECES * BLOCK + offsets
        rotated = rotate_keys(projected[:, :HEAD_DIM], positions)
        return jnp.concatenate([rotated, projected[:, HEAD_DIM:]], axis=1).astype(jnp.bfloat16)
    stacked = lax.map(recompute, jnp.arange(HITS, dtype=jnp.int32))
    prefix_cache = jnp.transpose(stacked, (1, 2, 0, 3)).reshape(KV_HEADS, 2 * HEAD_DIM, HITS * BLOCK)
    scale = HEAD_DIM ** (-0.5)
    prefix_len = PIECES * BLOCK
    pages_dev = ROWS_DEV * ROW_BLOCKS

    def decode(row):
        query = queries[row].astype(jnp.float32).reshape(KV_HEADS, QUERY_GROUP, HEAD_DIM)
        start = (row_prefix[row] * prefix_len).astype(jnp.int32)
        window = lax.dynamic_slice_in_dim(prefix_cache, start, prefix_len, 2).astype(jnp.float32)
        scores = jnp.einsum('kgd,kdt->kgt', query, window[:, :HEAD_DIM], precision=highest) * scale
        peak = lax.optimization_barrier(jnp.max(scores, axis=-1))
        weights = jnp.exp(scores - peak[..., None])
        mass = lax.optimization_barrier(jnp.sum(weights, axis=-1))
        rounded = lax.optimization_barrier(weights.astype(jnp.bfloat16)).astype(jnp.float32)
        prefix_out = jnp.einsum('kgt,kdt->kgd', rounded, window[:, HEAD_DIM:], precision=highest) / mass[..., None]
        prefix_lse = peak + jnp.log(mass)
        pages = row // ROWS_DEV * pages_dev + block_table[row]
        keys = cache_keys[:, pages].reshape(KV_HEADS, CONTEXT, HEAD_DIM).astype(jnp.float32)
        values = cache_values[:, pages].reshape(KV_HEADS, CONTEXT, HEAD_DIM).astype(jnp.float32)
        res_scores = jnp.einsum('kgd,ktd->kgt', query, keys, precision=highest) * scale
        valid = (jnp.arange(CONTEXT, dtype=jnp.int32) < row_length[row])[None, None, :]
        res_peak = lax.optimization_barrier(jnp.max(jnp.where(valid, res_scores, -jnp.inf), axis=-1))
        res_weights = jnp.where(valid, jnp.exp(res_scores - res_peak[..., None]), 0.0)
        res_mass = lax.optimization_barrier(jnp.sum(res_weights, axis=-1))
        res_rounded = lax.optimization_barrier(res_weights.astype(jnp.bfloat16)).astype(jnp.float32)
        res_sum = jnp.einsum('kgt,ktd->kgd', res_rounded, values, precision=highest)
        top = jnp.maximum(res_peak, prefix_lse)
        res_factor = jnp.exp(res_peak - top)
        pre_factor = jnp.exp(prefix_lse - top)
        numer = res_sum * res_factor[..., None] + prefix_out * pre_factor[..., None]
        denom = res_mass * res_factor + pre_factor
        return (numer / denom[..., None]).reshape(-1).astype(jnp.bfloat16)
    attended = lax.map(decode, jnp.arange(ROWS, dtype=jnp.int32))
    return (prefix_cache, attended)
```

```python
import functools
import math

import jax
import jax.numpy as jnp
import numpy as np
from jax import lax
from jax.experimental import pallas as pl
from jax.experimental.pallas import tpu as pltpu
from jax.sharding import PartitionSpec as P

HEAD_DIM = 128
QUERY_GROUP = 8
BLOCK = 128
PIECES = 4
BATCH = 4
LANES = 4
F32 = jnp.float32
BF16 = jnp.bfloat16
NN = (((1,), (0,)), ((), ()))
NT = (((1,), (1,)), ((), ()))


def rotation_tables():
    half = HEAD_DIM // 2
    freqs = np.exp(np.arange(half) * (-2.0 / HEAD_DIM) * math.log(500000.0))
    positions = np.arange(PIECES * BLOCK).reshape(PIECES, 1, BLOCK)
    angles = positions * freqs[None, :, None]
    return np.cos(angles).astype(np.float32), np.sin(angles).astype(np.float32)


def kernel(
    np_,
    nh,
    gb,
    hit_s,
    rowpref_s,
    rowlen_s,
    table_s,
    gain_ref,
    cos_ref,
    sin_ref,
    query_ref,
    x_hbm,
    w_hbm,
    keys_hbm,
    vals_hbm,
    cache_hbm,
    att_ref,
    hits_sm,
    rank_sm,
    x_v,
    w_v,
    keys_v,
    vals_v,
    xs_v,
    part_v,
    ring_v,
    ss_own,
    ss_v,
    kv_v,
    outbox,
    inbox,
    cache_v,
    own_q,
    q_v,
    pref_v,
    lse_v,
    msg_v,
    back_v,
    res_v,
    x_sem,
    w_sem,
    page_sem,
    ring_send,
    ring_recv,
    ss_sem,
    q_sem,
    box_sem,
    msg_sem,
    out_sem,
):
    me = lax.axis_index("pool")
    z = lax.axis_index("head")
    nb = gb // BATCH
    last = nh - 2
    steps = nh - 1
    dim = x_hbm.shape[2] * nh
    rows_dev = rowlen_s.shape[0]
    row_blocks = table_s.shape[1]
    qrows = rows_dev * QUERY_GROUP
    hd = HEAD_DIM
    scale = hd ** (-0.5)
    up = lax.rem(z + 1, nh)
    down = lax.rem(z + nh - 1, nh)
    half = BATCH // 2 * BLOCK
    sub8 = lax.broadcasted_iota(jnp.int32, (8, hd), 0)
    lane_rows = half // LANES

    def w_copy(h):
        return pltpu.make_async_copy(
            w_hbm.at[:, pl.ds(pl.multiple_of(h * 2 * hd, 2 * hd), 2 * hd)], w_v.at[h], w_sem.at[h]
        )

    x_copy = pltpu.make_async_copy(x_hbm, x_v, x_sem)
    x_copy.start()
    for s in range(nh // 2):
        w_copy(lax.rem(z + nh - 1 - s, nh)).start()
        if s + 1 < nh - 1 - s:
            w_copy(lax.rem(z + 1 + s, nh)).start()
    w_copy(z).start()
    key_copy = pltpu.make_async_copy(keys_hbm, keys_v, page_sem.at[0])
    val_copy = pltpu.make_async_copy(vals_hbm, vals_v, page_sem.at[1])
    key_copy.start()
    val_copy.start()

    query = query_ref[...].astype(F32)
    stacked = jnp.concatenate([query[:, j * hd : (j + 1) * hd] for j in range(QUERY_GROUP)], axis=0)
    own_q[...] = stacked.astype(BF16)
    q_v[me] = stacked.astype(BF16)

    barrier = pltpu.get_barrier_semaphore()

    def greet_pool(i, c):
        pl.semaphore_signal(barrier, inc=1, device_id={"pool": lax.rem(me + i, np_)})
        return c

    lax.fori_loop(1, np_, greet_pool, 0)

    def greet_head(i, c):
        pl.semaphore_signal(barrier, inc=1, device_id={"head": lax.rem(z + i, nh)})
        return c

    lax.fori_loop(1, nh, greet_head, 0)

    def find(rel, carry):
        count, found = carry
        group = lax.rem(me + 1 + rel, np_)
        hit = jnp.int32(-1)
        for t in range(gb):
            k = group * gb + t
            hit = jnp.where(hit_s[k] // gb == me, k, hit)
        present = hit >= 0
        rank_sm[rel] = jnp.minimum(count, gb - 1)
        found = tuple(
            jnp.where(jnp.logical_and(present, count == i), hit, found[i]) for i in range(gb)
        )
        return count + present.astype(jnp.int32), found

    _, found = lax.fori_loop(0, np_, find, (jnp.int32(0), (jnp.int32(0),) * gb))
    for i in range(gb):
        hits_sm[i] = found[i]

    pl.semaphore_wait(barrier, np_ - 1 + nh - 1)

    def q_copy(source, peer):
        return pltpu.make_async_remote_copy(
            src_ref=own_q,
            dst_ref=q_v.at[source],
            send_sem=q_sem.at[0, peer],
            recv_sem=q_sem.at[1, source],
            device_id={"pool": peer},
        )

    def for_peers(mine, n, act):
        def one(i, c):
            act(lax.rem(mine + i, n))
            return c

        lax.fori_loop(1, n, one, 0)

    def prepare(b):
        for t in range(BATCH):
            wide = x_v[hit_s[hits_sm[b * BATCH + t]] % gb].astype(F32)
            xs_v[b % 2, t // 2, (t % 2) * BLOCK : (t % 2 + 1) * BLOCK, :] = (
                wide * gain_ref[...]
            ).astype(BF16)
            square = wide * wide
            fold = square[:, :hd]
            for c in range(1, square.shape[1] // hd):
                fold = fold + square[:, c * hd : (c + 1) * hd]
            sums = lax.dot_general(
                jnp.ones((8, hd), F32),
                fold,
                NT,
                precision=lax.Precision.HIGHEST,
                preferred_element_type=F32,
            )
            ss_own[b // 2] = jnp.where(sub8 == b % 2 * BATCH + t, sums, ss_own[b // 2])

    def ss_copy(pair, source, peer):
        return pltpu.make_async_remote_copy(
            src_ref=ss_own.at[pair],
            dst_ref=ss_v.at[pair, source],
            send_sem=ss_sem.at[0, pair, peer],
            recv_sem=ss_sem.at[1, pair, source],
            device_id={"head": peer},
        )

    def ss_send(pair):
        for_peers(z, nh, lambda peer: ss_copy(pair, z, peer).start())

    def ring_copy(way, b, s, lane, parity):
        return pltpu.make_async_remote_copy(
            src_ref=ring_v.at[way, b, s, lane],
            dst_ref=ring_v.at[way, b, s + 1, lane],
            send_sem=ring_send.at[way, lane, parity],
            recv_sem=ring_recv.at[way, b, s, lane],
            device_id={"head": up if way == 0 else down},
        )

    def multiply(way, b, h):
        return lax.dot_general(xs_v[b % 2, way], w_v[h], NN, preferred_element_type=F32)

    def finish(way, b):
        part_v[way] = multiply(way, b, z)
        for t in range(BATCH // 2):
            i = b * BATCH + way * (BATCH // 2) + t
            per = LANES // (BATCH // 2)
            for lane in range(t * per, (t + 1) * per):
                ring_copy(way, b, last, lane, 0).wait_recv()
            total = part_v[way, t * BLOCK : (t + 1) * BLOCK, :] + jnp.concatenate(
                [ring_v[way, b, last + 1, lane] for lane in range(t * per, (t + 1) * per)], axis=0
            ).astype(F32)
            tiles = ss_own[b // 2]
            for other in range(1, nh):
                tiles = tiles + ss_v[b // 2, lax.rem(z + other, nh)]
            row = b % 2 * BATCH + way * 2 + t
            squares = jnp.sum(jnp.where(sub8 == row, tiles, 0.0), axis=0, keepdims=True)
            normed = jnp.transpose(total) * lax.rsqrt(squares / dim + 1e-05)
            first = normed[: hd // 2]
            second = normed[hd // 2 : hd]
            piece = hits_sm[i] % PIECES
            cosine = cos_ref[piece]
            sine = sin_ref[piece]
            kv_v[i] = jnp.concatenate(
                [first * cosine - second * sine, second * cosine + first * sine, normed[hd:]],
                axis=0,
            ).astype(BF16)

    def box_copy(rel, source):
        return pltpu.make_async_remote_copy(
            src_ref=outbox.at[rel],
            dst_ref=inbox.at[source],
            send_sem=box_sem.at[0, rel],
            recv_sem=box_sem.at[1, source],
            device_id={"pool": lax.rem(me + 1 + rel, np_)},
        )

    def box_send(start, stop):
        def one(rel, c):
            outbox[rel] = kv_v[rank_sm[rel]]
            box_copy(rel, me).start()
            return c

        lax.fori_loop(start, stop, one, 0)

    def attend(b, c):
        wide = 4
        q = q_v[pl.ds(c * wide, wide)].reshape(wide * qrows, hd)
        rowpref = jnp.broadcast_to(
            pref_v[pl.ds(c * wide, wide)][:, None], (wide, QUERY_GROUP, rows_dev, hd)
        ).reshape(wide * qrows, hd)
        scores = jnp.zeros((wide * qrows, hd), F32)
        masks = []
        for t in range(BATCH):
            mask = rowpref == hits_sm[b * BATCH + t] // PIECES
            masks.append(mask)
            s = lax.dot_general(q, kv_v[b * BATCH + t, :hd], NN, preferred_element_type=F32)
            scores = jnp.where(mask, s, scores)
        scores = scores * scale
        peak = jnp.max(scores, axis=1, keepdims=True)
        weights = jnp.exp(scores - peak)
        mass = jnp.sum(weights, axis=1, keepdims=True)
        total = jnp.zeros((wide * qrows, hd), F32)
        for t in range(BATCH):
            total = total + lax.dot_general(
                jnp.where(masks[t], weights, 0.0).astype(BF16),
                kv_v[b * BATCH + t, hd:],
                NT,
                preferred_element_type=F32,
            )
        hit = functools.reduce(jnp.logical_or, masks)
        out = total / mass
        lse = jnp.broadcast_to(peak + jnp.log(mass), (wide * qrows, hd))
        rows = pl.ds(c * wide, wide)
        old = msg_v[rows, :qrows, :].reshape(wide * qrows, hd).astype(F32)
        msg_v[rows, :qrows, :] = jnp.where(hit, out, old).astype(BF16).reshape(wide, qrows, hd)
        old = lse_v[rows].reshape(wide * qrows, hd)
        lse_v[rows] = jnp.where(hit, lse, old).reshape(wide, qrows, hd)

    row_id = lax.rem(lax.broadcasted_iota(jnp.int32, (qrows, hd), 0), rows_dev)

    def resident(r):
        q = own_q[...]
        pages = [table_s[r, i] for i in range(row_blocks)]
        scores = (
            jnp.concatenate(
                [
                    lax.dot_general(q, keys_v[page], NT, preferred_element_type=F32)
                    for page in pages
                ],
                axis=1,
            )
            * scale
        )
        token = lax.broadcasted_iota(jnp.int32, scores.shape, 1)
        valid = token < rowlen_s[r]
        peak = jnp.max(jnp.where(valid, scores, -jnp.inf), axis=1, keepdims=True)
        weights = jnp.where(valid, jnp.exp(scores - peak), 0.0)
        mass = jnp.sum(weights, axis=1, keepdims=True)
        rounded = weights.astype(BF16)
        total = jnp.zeros((qrows, hd), F32)
        for i, page in enumerate(pages):
            total = total + lax.dot_general(
                rounded[:, i * BLOCK : (i + 1) * BLOCK],
                vals_v[page],
                NN,
                preferred_element_type=F32,
            )
        mine = row_id == r
        res_v[0] = jnp.where(mine, total, res_v[0])
        res_v[1] = jnp.where(mine, peak, res_v[1])
        res_v[2] = jnp.where(mine, mass, res_v[2])

    x_copy.wait()
    prepare(0)
    for h in range(nh):
        w_copy(h).wait()
    key_copy.wait()
    val_copy.wait()

    per_step = -(-rows_dev // last)
    att_from = min(3, last)
    chunks = np_ // 4
    per_att = -(-chunks // (last - att_from + 1))

    def ring_step(b, s, first):
        g = b * steps + s
        heads = (lax.rem(z + 2 * nh - 1 - s, nh), lax.rem(z + 1 + s, nh))
        parity = lax.rem(g, 2)
        for way in range(2):
            part_v[way] = multiply(way, b, heads[way])
        for lane in range(LANES):
            rows = slice(lane * lane_rows, (lane + 1) * lane_rows)
            for way in range(2):
                if first:
                    ring_v[way, b, 0, lane] = part_v[way, rows, :].astype(BF16)
                else:
                    ring_copy(way, b, s - 1, lane, parity).wait_recv()
                    ring_v[way, b, s, lane] = (
                        ring_v[way, b, s, lane].astype(F32) + part_v[way, rows, :]
                    ).astype(BF16)
                if first and b > 0:
                    ring_copy(way, b, s, lane, parity).wait_send()
                if not first and b > 0:
                    ring_copy(way, b, s, lane, parity).wait_send()
                if not first and b == 0:

                    @pl.when(s >= 2)
                    def _():
                        ring_copy(way, b, s, lane, parity).wait_send()

                ring_copy(way, b, s, lane, parity).start()

    for b in range(nb):
        ring_step(b, 0, True)
        if b == 0:
            for_peers(me, np_, lambda peer: q_copy(me, peer).start())
            sub = lax.broadcasted_iota(jnp.int32, (rows_dev, hd), 0)

            def fill(i, c):
                tile = jnp.zeros((rows_dev, hd), jnp.int32)
                for r in range(rows_dev):
                    tile = jnp.where(sub == r, rowpref_s[i * rows_dev + r], tile)
                pref_v[i] = tile
                return c

            lax.fori_loop(0, np_, fill, 0)
        if b % 2 == 1:
            for_peers(z, nh, lambda peer, pair=b // 2: ss_copy(pair, peer, peer).wait_recv())

        def step(s, carry):
            ring_step(b, s, False)
            if b == 0:
                for e in range(per_step):
                    r = (s - 1) * per_step + e

                    @pl.when(r < rows_dev)
                    def _():
                        resident(r)

            else:

                @pl.when(s == 1)
                def _():
                    finish(0, b - 1)

                @pl.when(s == 2)
                def _():
                    finish(1, b - 1)
                    box_send((b - 1) * BATCH, b * BATCH)

                for e in range(per_att):
                    c = (s - att_from) * per_att + e

                    @pl.when(jnp.logical_and(s >= att_from, c < chunks))
                    def _():
                        attend(b - 1, c)

            if b + 1 < nb:

                @pl.when(s == 2)
                def _():
                    prepare(b + 1)

            return carry

        lax.fori_loop(1, steps, step, 0)
        if b == 0:
            for_peers(me, np_, lambda peer: q_copy(peer, peer).wait_recv())
        if b % 2 == 0:
            ss_send(b // 2)

    b = nb - 1
    finish(0, b)
    finish(1, b)
    early = min((nb - 1) * BATCH + 6, np_ - 1)
    box_send((nb - 1) * BATCH, early)

    def msg_copy(source, peer):
        return pltpu.make_async_remote_copy(
            src_ref=msg_v.at[peer],
            dst_ref=back_v.at[source],
            send_sem=msg_sem.at[0, peer],
            recv_sem=msg_sem.at[1, source],
            device_id={"pool": peer},
        )

    lane_id = lax.broadcasted_iota(jnp.int32, (qrows, hd), 1)
    diagonal = lane_id == lax.broadcasted_iota(jnp.int32, (qrows, hd), 0)
    sub16 = lax.broadcasted_iota(jnp.int32, (16, hd), 0)

    def last_chunk(i, carry):
        c = lax.rem(me // 4 + i, chunks)
        attend(b, c)
        for e in range(4):
            peer = c * 4 + e
            row = jnp.sum(jnp.where(diagonal, lse_v[peer], 0.0), axis=0, keepdims=True)
            high = row.astype(BF16).astype(F32)
            rest = row - high
            middle = rest.astype(BF16).astype(F32)
            low = rest - middle
            msg_v[peer, qrows:, :] = jnp.where(
                sub16 == 0,
                high,
                jnp.where(sub16 == 1, middle, jnp.where(sub16 == 2, low, 0.0)),
            ).astype(BF16)

            @pl.when(peer != me)
            def _():
                msg_copy(me, peer).start()

        return carry

    lax.fori_loop(0, chunks, last_chunk, 0)
    box_send(early, np_ - 1)

    for_peers(me, np_, lambda peer: msg_copy(peer, peer).wait_recv())
    outs = []
    lses = []
    row_lane = lax.rem(lax.broadcasted_iota(jnp.int32, (1, hd), 1), rows_dev)
    for i in range(PIECES):
        out = jnp.zeros((qrows, hd), F32)
        line = jnp.zeros((1, hd), F32)
        for r in range(rows_dev):
            source = hit_s[rowpref_s[me * rows_dev + r] * PIECES + i] // gb
            note = jnp.where(source == me, msg_v[me], back_v[source]).astype(F32)
            out = jnp.where(row_id == r, note[:qrows], out)
            text = jnp.sum(note[qrows:], axis=0, keepdims=True)
            line = jnp.where(row_lane == r, text, line)
        outs.append(out)
        lses.append(jnp.sum(jnp.where(diagonal, line, 0.0), axis=1, keepdims=True))
    res_peak = res_v[1]
    top = res_peak
    for lse in lses:
        top = jnp.maximum(top, lse)
    factor = jnp.exp(res_peak - top)
    numer = res_v[0] * factor
    denom = res_v[2] * factor
    for out, lse in zip(outs, lses):
        factor = jnp.exp(lse - top)
        numer = numer + out * factor
        denom = denom + factor
    attended = numer / denom
    att_ref[...] = jnp.concatenate(
        [attended[j * rows_dev : (j + 1) * rows_dev] for j in range(QUERY_GROUP)], axis=1
    ).astype(BF16)

    for_peers(me, np_, lambda peer: box_copy(0, peer).wait_recv())
    own_kv = kv_v[rank_sm[np_ - 1]]
    for j in range(gb):
        source = hit_s[me * gb + j] // gb
        cache_v[:, j * BLOCK : (j + 1) * BLOCK] = jnp.where(source == me, own_kv, inbox[source])
    out_copy = pltpu.make_async_copy(cache_v, cache_hbm, out_sem)
    out_copy.start()

    def drain(rel, c):
        box_copy(rel, me).wait_send()
        return c

    lax.fori_loop(0, np_ - 1, drain, 0)
    for_peers(me, np_, lambda peer: q_copy(me, peer).wait_send())
    for_peers(me, np_, lambda peer: msg_copy(me, peer).wait_send())
    for i in range(nb // 2):
        for_peers(z, nh, lambda peer: ss_copy(i, z, peer).wait_send())
    for parity in range(2):
        for lane in range(LANES):
            for way in range(2):
                ring_copy(way, 0, 0, lane, parity).wait_send()
    out_copy.wait()


def shards(
    pool_rows,
    hit_owner,
    norm_gain,
    kv_weight,
    queries,
    row_prefix,
    row_length,
    block_table,
    cache_keys,
    cache_values,
):
    np_ = lax.axis_size("pool")
    nh = lax.axis_size("head")
    gb = hit_owner.shape[0] // np_
    nb = gb // BATCH
    rows_dev = queries.shape[0]
    qrows = rows_dev * QUERY_GROUP
    features = pool_rows.shape[1]
    hd = HEAD_DIM
    cosine, sine = rotation_tables()
    smem = pl.BlockSpec(memory_space=pltpu.SMEM)
    vmem = pl.BlockSpec(memory_space=pltpu.VMEM)
    hbm = pl.BlockSpec(memory_space=pl.ANY)
    dma = pltpu.SemaphoreType.DMA
    half = BATCH // 2 * BLOCK
    cache, attended = pl.pallas_call(
        functools.partial(kernel, np_, nh, gb),
        out_shape=(
            jax.ShapeDtypeStruct((2 * hd, gb * BLOCK), BF16),
            jax.ShapeDtypeStruct(queries.shape, BF16),
        ),
        in_specs=[smem] * 4 + [vmem] * 4 + [hbm] * 4,
        out_specs=(hbm, vmem),
        scratch_shapes=[
            pltpu.SMEM((gb,), jnp.int32),
            pltpu.SMEM((np_,), jnp.int32),
            pltpu.VMEM((gb, BLOCK, features), BF16),
            pltpu.VMEM((nh, features, 2 * hd), BF16),
            pltpu.VMEM(cache_keys.shape[1:], BF16),
            pltpu.VMEM(cache_values.shape[1:], BF16),
            pltpu.VMEM((2, 2, half, features), BF16),
            pltpu.VMEM((2, half, 2 * hd), F32),
            pltpu.VMEM((2, nb, nh, LANES, half // LANES, 2 * hd), BF16),
            pltpu.VMEM((nb // 2, 8, BLOCK), F32),
            pltpu.VMEM((nb // 2, nh, 8, BLOCK), F32),
            pltpu.VMEM((gb, 2 * hd, BLOCK), BF16),
            pltpu.VMEM((np_ - 1, 2 * hd, BLOCK), BF16),
            pltpu.VMEM((np_, 2 * hd, BLOCK), BF16),
            pltpu.VMEM((2 * hd, gb * BLOCK), BF16),
            pltpu.VMEM((qrows, hd), BF16),
            pltpu.VMEM((np_, qrows, hd), BF16),
            pltpu.VMEM((np_, rows_dev, hd), jnp.int32),
            pltpu.VMEM((np_, qrows, hd), F32),
            pltpu.VMEM((np_, qrows + 16, hd), BF16),
            pltpu.VMEM((np_, qrows + 16, hd), BF16),
            pltpu.VMEM((3, qrows, hd), F32),
            dma,
            dma((nh,)),
            dma((2,)),
            dma((2, LANES, 2)),
            dma((2, nb, nh - 1, LANES)),
            dma((2, nb // 2, nh)),
            dma((2, np_)),
            dma((2, np_)),
            dma((2, np_)),
            dma,
        ],
        compiler_params=pltpu.CompilerParams(
            collective_id=0, has_side_effects=True, vmem_limit_bytes=56 * 2**20
        ),
    )(
        hit_owner,
        row_prefix,
        row_length,
        block_table,
        norm_gain.reshape(1, features),
        jnp.asarray(cosine),
        jnp.asarray(sine),
        queries,
        pool_rows.reshape(gb, BLOCK, features),
        kv_weight,
        cache_keys[0],
        cache_values[0],
    )
    return cache[None], attended


def solution(mesh):
    return jax.shard_map(
        shards,
        mesh=mesh,
        in_specs=(
            P("pool", "head"),
            P(),
            P("head"),
            P("head", None),
            P("pool", "head"),
            P(),
            P("pool"),
            P("pool", None),
            P("head", "pool", None, None),
            P("head", "pool", None, None),
        ),
        out_specs=(P("head", None, "pool"), P("pool", "head")),
        check_vma=False,
    )
```

```python
import functools
import math

import jax
import jax.numpy as jnp
import numpy as np
from jax import lax
from jax.experimental import pallas as pl
from jax.experimental.pallas import tpu as pltpu
from jax.sharding import PartitionSpec as P

HEAD_DIM = 128
QUERY_GROUP = 8
BLOCK = 128
PIECES = 4
BATCH = 4
LANES = 2
F32 = jnp.float32
BF16 = jnp.bfloat16
NN = (((1,), (0,)), ((), ()))
NT = (((1,), (1,)), ((), ()))


def rotation_tables():
    half = HEAD_DIM // 2
    freqs = np.exp(np.arange(half) * (-2.0 / HEAD_DIM) * math.log(500000.0))
    positions = np.arange(PIECES * BLOCK).reshape(PIECES, 1, BLOCK)
    angles = positions * freqs[None, :, None]
    return np.cos(angles).astype(np.float32), np.sin(angles).astype(np.float32)


def offsets(np_):
    wide = 4 if np_ >= 32 else 2
    high = np_ // (2 * wide)

    def key(step):
        y, x, core = step
        far_y, far_x = min(y, high - y), min(x, wide - x)
        straight = far_y == 0 or far_x == 0
        return (-(far_y + far_x), not straight, core if far_y + far_x else -core, y, x)

    return wide, high, sorted(
        ((y, x, core) for y in range(high) for x in range(wide) for core in range(2)), key=key
    )


def kernel(
    np_,
    nh,
    gb,
    hit_s,
    rowpref_s,
    rowlen_s,
    table_s,
    gain_ref,
    cos_ref,
    sin_ref,
    query_ref,
    x_hbm,
    w_hbm,
    keys_hbm,
    vals_hbm,
    cache_hbm,
    att_ref,
    hits_sm,
    rank_sm,
    x_v,
    w_v,
    keys_v,
    vals_v,
    xs_v,
    part_v,
    ring_v,
    ss_own,
    ss_v,
    kv_v,
    wide_v,
    outbox,
    inbox,
    cache_v,
    own_q,
    q_v,
    pref_v,
    lse_v,
    msg_v,
    back_v,
    res_v,
    x_sem,
    w_sem,
    page_sem,
    ring_send,
    ring_recv,
    ss_sem,
    q_sem,
    box_sem,
    msg_sem,
    out_sem,
):
    me = lax.axis_index("pool")
    z = lax.axis_index("head")
    nb = gb // BATCH
    last = nh - 2
    steps = nh - 1
    dim = x_hbm.shape[2] * nh
    rows_dev = rowlen_s.shape[0]
    row_blocks = table_s.shape[0]
    qrows = rows_dev * QUERY_GROUP
    hd = HEAD_DIM
    scale = hd ** (-0.5)
    up = lax.rem(z + 1, nh)
    down = lax.rem(z + nh - 1, nh)
    half = BATCH // 2 * BLOCK
    sub8 = lax.broadcasted_iota(jnp.int32, (8, hd), 0)
    lane_rows = half // LANES

    wide_x, high_y, hops = offsets(np_)
    core = lax.rem(me, 2)
    at_x = lax.rem(lax.div(me, 2), wide_x)
    at_y = lax.div(me, 2 * wide_x)

    def dest(rel):
        y, x, c = hops[rel]
        return (lax.rem(at_y + y, high_y) * wide_x + lax.rem(at_x + x, wide_x)) * 2 + lax.rem(
            core + c, 2
        )

    def w_copy(h):
        return pltpu.make_async_copy(
            w_hbm.at[:, pl.ds(pl.multiple_of(h * 2 * hd, 2 * hd), 2 * hd)], w_v.at[h], w_sem.at[h]
        )

    x_copy = pltpu.make_async_copy(x_hbm, x_v, x_sem)
    x_copy.start()
    for s in range(nh // 2):
        w_copy(lax.rem(z + nh - 1 - s, nh)).start()
        if s + 1 < nh - 1 - s:
            w_copy(lax.rem(z + 1 + s, nh)).start()
    w_copy(z).start()
    key_copy = pltpu.make_async_copy(keys_hbm, keys_v, page_sem.at[0])
    val_copy = pltpu.make_async_copy(vals_hbm, vals_v, page_sem.at[1])
    key_copy.start()
    val_copy.start()

    query = query_ref[...].astype(F32)
    stacked = jnp.concatenate([query[:, j * hd : (j + 1) * hd] for j in range(QUERY_GROUP)], axis=0)
    own_q[...] = stacked.astype(BF16)
    q_v[me] = stacked.astype(BF16)

    barrier = pltpu.get_barrier_semaphore()

    def greet_pool(i, c):
        pl.semaphore_signal(barrier, inc=1, device_id={"pool": lax.rem(me + i, np_)})
        return c

    lax.fori_loop(1, np_, greet_pool, 0)

    def greet_head(i, c):
        pl.semaphore_signal(barrier, inc=1, device_id={"head": lax.rem(z + i, nh)})
        return c

    lax.fori_loop(1, nh, greet_head, 0)

    count = jnp.int32(0)
    found = [jnp.int32(0)] * gb
    for rel in range(np_):
        base = dest(rel) * gb
        hit = jnp.int32(-1)
        for t in range(gb):
            holder = hit_s[base + t]
            mine = jnp.logical_and(holder >= me * gb, holder < me * gb + gb)
            hit = jnp.where(mine, base + t, hit)
        present = hit >= 0
        rank_sm[rel] = jnp.minimum(count, gb - 1)
        for i in range(max(0, rel - (np_ - gb)), min(rel + 1, gb)):
            found[i] = jnp.where(jnp.logical_and(present, count == i), hit, found[i])
        count = count + present.astype(jnp.int32)
    for i in range(gb):
        hits_sm[i] = found[i]

    def q_copy(source, peer):
        return pltpu.make_async_remote_copy(
            src_ref=own_q,
            dst_ref=q_v.at[source],
            send_sem=q_sem.at[0, peer],
            recv_sem=q_sem.at[1, source],
            device_id={"pool": peer},
        )

    def for_peers(mine, n, act):
        def one(i, c):
            act(lax.rem(mine + i, n))
            return c

        lax.fori_loop(1, n, one, 0)

    def prepare(b):
        for t in range(BATCH):
            wide = x_v[hit_s[hits_sm[b * BATCH + t]] % gb].astype(F32)
            xs_v[b, t // 2, (t % 2) * BLOCK : (t % 2 + 1) * BLOCK, :] = (
                wide * gain_ref[...]
            ).astype(BF16)
            square = wide * wide
            fold = square[:, :hd]
            for c in range(1, square.shape[1] // hd):
                fold = fold + square[:, c * hd : (c + 1) * hd]
            sums = lax.dot_general(
                jnp.ones((8, hd), F32),
                fold,
                NT,
                precision=lax.Precision.HIGHEST,
                preferred_element_type=F32,
            )
            ss_own[b // 2] = jnp.where(sub8 == b % 2 * BATCH + t, sums, ss_own[b // 2])

    def ss_copy(pair, source, peer):
        return pltpu.make_async_remote_copy(
            src_ref=ss_own.at[pair],
            dst_ref=ss_v.at[pair, source],
            send_sem=ss_sem.at[0, pair, peer],
            recv_sem=ss_sem.at[1, pair, source],
            device_id={"head": peer},
        )

    def ss_send(pair):
        for_peers(z, nh, lambda peer: ss_copy(pair, z, peer).start())

    def ring_copy(way, b, s, lane, parity):
        return pltpu.make_async_remote_copy(
            src_ref=ring_v.at[way, b, s, lane],
            dst_ref=ring_v.at[way, b, s + 1, lane],
            send_sem=ring_send.at[way, b, lane, parity],
            recv_sem=ring_recv.at[way, b, s, lane],
            device_id={"head": up if way == 0 else down},
        )

    def multiply(way, b, h):
        return lax.dot_general(xs_v[b, way], w_v[h], NN, preferred_element_type=F32)

    def finish(way, b):
        part_v[way] = multiply(way, b, z)
        for t in range(BATCH // 2):
            i = b * BATCH + way * (BATCH // 2) + t
            per = LANES // (BATCH // 2)
            for lane in range(t * per, (t + 1) * per):
                ring_copy(way, b, last, lane, 0).wait_recv()
            total = part_v[way, t * BLOCK : (t + 1) * BLOCK, :] + jnp.concatenate(
                [ring_v[way, b, last + 1, lane] for lane in range(t * per, (t + 1) * per)], axis=0
            ).astype(F32)
            tiles = ss_own[b // 2]
            for other in range(1, nh):
                tiles = tiles + ss_v[b // 2, lax.rem(z + other, nh)]
            row = b % 2 * BATCH + way * 2 + t
            squares = jnp.sum(jnp.where(sub8 == row, tiles, 0.0), axis=0, keepdims=True)
            normed = jnp.transpose(total) * lax.rsqrt(squares / dim + 1e-05)
            first = normed[: hd // 2]
            second = normed[hd // 2 : hd]
            piece = hits_sm[i] % PIECES
            cosine = cos_ref[piece]
            sine = sin_ref[piece]
            both = jnp.concatenate(
                [first * cosine - second * sine, second * cosine + first * sine, normed[hd:]],
                axis=0,
            ).astype(BF16)
            kv_v[i] = both
            place = way * (BATCH // 2) + t
            wide_v[b, :, place * BLOCK : (place + 1) * BLOCK] = both

    def box_copy(rel, source):
        return pltpu.make_async_remote_copy(
            src_ref=outbox.at[rel],
            dst_ref=inbox.at[source],
            send_sem=box_sem.at[0, rel],
            recv_sem=box_sem.at[1, source],
            device_id={"pool": dest(rel)},
        )

    def box_send(start, stop):
        for rel in range(start, stop):
            outbox[rel] = kv_v[rank_sm[rel]]
            box_copy(rel, me).start()

    def attend(b, c):
        wide = 4
        q = q_v[pl.ds(c * wide, wide)].reshape(wide * qrows, hd)
        rowpref = jnp.broadcast_to(
            pref_v[pl.ds(c * wide, wide)][:, None], (wide, QUERY_GROUP, rows_dev, hd)
        ).reshape(wide * qrows, hd)
        every = lax.dot_general(q, wide_v[b, :hd], NN, preferred_element_type=F32)
        masks = [rowpref == hits_sm[b * BATCH + t] // PIECES for t in range(BATCH)]
        scores = every[:, :BLOCK]
        for t in range(1, BATCH):
            scores = jnp.where(masks[t], every[:, t * BLOCK : (t + 1) * BLOCK], scores)
        scores = scores * scale
        peak = jnp.max(scores, axis=1, keepdims=True)
        weights = jnp.exp(scores - peak)
        mass = jnp.sum(weights, axis=1, keepdims=True)
        spread = jnp.concatenate(
            [jnp.where(masks[t], weights, 0.0).astype(BF16) for t in range(BATCH)], axis=1
        )
        total = lax.dot_general(spread, wide_v[b, hd:], NT, preferred_element_type=F32)
        hit = functools.reduce(jnp.logical_or, masks)
        out = total / mass
        lse = jnp.broadcast_to(peak + jnp.log(mass), (wide * qrows, hd))
        rows = pl.ds(c * wide, wide)
        old = msg_v[rows, :qrows, :].reshape(wide * qrows, hd).astype(F32)
        msg_v[rows, :qrows, :] = jnp.where(hit, out, old).astype(BF16).reshape(wide, qrows, hd)
        old = lse_v[rows].reshape(wide * qrows, hd)
        lse_v[rows] = jnp.where(hit, lse, old).reshape(wide, qrows, hd)

    row_id = lax.rem(lax.broadcasted_iota(jnp.int32, (qrows, hd), 0), rows_dev)

    def resident(r):
        q = own_q[...]
        pages = [table_s[i, r] for i in range(row_blocks)]
        scores = (
            jnp.concatenate(
                [
                    lax.dot_general(q, keys_v[page], NT, preferred_element_type=F32)
                    for page in pages
                ],
                axis=1,
            )
            * scale
        )
        token = lax.broadcasted_iota(jnp.int32, scores.shape, 1)
        valid = token < rowlen_s[r]
        peak = jnp.max(jnp.where(valid, scores, -jnp.inf), axis=1, keepdims=True)
        weights = jnp.where(valid, jnp.exp(scores - peak), 0.0)
        mass = jnp.sum(weights, axis=1, keepdims=True)
        rounded = weights.astype(BF16)
        total = jnp.zeros((qrows, hd), F32)
        for i, page in enumerate(pages):
            total = total + lax.dot_general(
                rounded[:, i * BLOCK : (i + 1) * BLOCK],
                vals_v[page],
                NN,
                preferred_element_type=F32,
            )
        mine = row_id == r
        res_v[0] = jnp.where(mine, total, res_v[0])
        res_v[1] = jnp.where(mine, peak, res_v[1])
        res_v[2] = jnp.where(mine, mass, res_v[2])

    chunks = np_ // 4

    def ring_step(b, s):
        heads = (lax.rem(z + 2 * nh - 1 - s, nh), lax.rem(z + 1 + s, nh))
        first = s == 0
        parity = s % 2
        for way in range(2):
            part_v[way] = multiply(way, b, heads[way])
        if b == 0 and s == 0:
            pl.semaphore_wait(barrier, np_ - 1 + nh - 1)
        for lane in range(LANES):
            rows = slice(lane * lane_rows, (lane + 1) * lane_rows)
            for way in range(2):
                if first:
                    ring_v[way, b, 0, lane] = part_v[way, rows, :].astype(BF16)
                else:
                    ring_copy(way, b, s - 1, lane, parity).wait_recv()
                    ring_v[way, b, s, lane] = (
                        ring_v[way, b, s, lane].astype(F32) + part_v[way, rows, :]
                    ).astype(BF16)

                    if s >= 2:
                        ring_copy(way, b, s, lane, parity).wait_send()

                ring_copy(way, b, s, lane, parity).start()

    def ring_drain(b):
        for way in range(2):
            for lane in range(LANES):
                for parity in range(2):
                    ring_copy(way, b, 0, lane, parity).wait_send()

    def attend_all(b, start, stop):
        def one(c, carry):
            attend(b, c)
            return carry

        lax.fori_loop(start, stop, one, 0)

    def resident_rows(start, stop):
        def one(r, carry):
            resident(r)
            return carry

        lax.fori_loop(start, stop, one, 0)

    def ss_wait(pair):
        for_peers(z, nh, lambda peer: ss_copy(pair, peer, peer).wait_recv())

    def start_queries():
        for_peers(me, np_, lambda peer: q_copy(me, peer).start())
        sub = lax.broadcasted_iota(jnp.int32, (rows_dev, hd), 0)

        def fill(i, c):
            tile = jnp.zeros((rows_dev, hd), jnp.int32)
            for r in range(rows_dev):
                tile = jnp.where(sub == r, rowpref_s[i * rows_dev + r], tile)
            pref_v[i] = tile
            return c

        lax.fori_loop(0, np_, fill, 0)

    def finish_both(b):
        if b % 2 == 0:
            ss_wait(b // 2)
        else:
            for_peers(z, nh, lambda peer: ss_copy(b // 2, z, peer).wait_send())
        if b > 0:
            ring_drain(b - 1)
        finish(0, b)
        finish(1, b)
        if b < nb - 1:
            box_send(b * BATCH, (b + 1) * BATCH)

    begin = [(b // 2) * steps + (b % 2) * 2 for b in range(nb)]
    total_rounds = begin[-1] + steps
    work = {r: [] for r in range(total_rounds)}
    work[0] += [lambda: prepare(1)]
    work[2] += [start_queries]
    for b in range(1, nb):
        ready = begin[b] - 1
        if b > 1:
            work[ready].append(functools.partial(prepare, b))
        if b % 2 == 1:
            work[ready].append(functools.partial(ss_send, b // 2))
    free = [r for r in range(1, begin[0] + steps)]
    for i, r in enumerate(free):
        lo, hi = i * rows_dev // len(free), (i + 1) * rows_dev // len(free)
        if lo < hi:
            work[r].append(functools.partial(resident_rows, lo, hi))
    work[free[-1]].append(lambda: for_peers(me, np_, lambda peer: q_copy(peer, peer).wait_recv()))
    work[free[-1]].append(lambda: for_peers(me, np_, lambda peer: q_copy(me, peer).wait_send()))
    for b in range(nb - 1):
        done = min(begin[b] + steps, total_rounds - 2)
        after = [r for r in range(done + 1, min(done + 3, total_rounds))]
        work[done].append(functools.partial(finish_both, b))
        for i, r in enumerate(after):
            lo, hi = i * chunks // len(after), (i + 1) * chunks // len(after)
            work[r].append(functools.partial(attend_all, b, lo, hi))
    x_copy.wait()
    prepare(0)
    for h in range(nh):
        w_copy(h).wait()
    key_copy.wait()
    val_copy.wait()
    for r in range(total_rounds):
        for b in range(nb):
            if begin[b] <= r < begin[b] + steps:
                ring_step(b, r - begin[b])
        for task in work[r]:
            task()

    b = nb - 1
    finish_both(b)
    early = min((nb - 1) * BATCH + 6, np_ - 1)
    box_send((nb - 1) * BATCH, early)

    def msg_copy(source, peer):
        return pltpu.make_async_remote_copy(
            src_ref=msg_v.at[peer],
            dst_ref=back_v.at[source],
            send_sem=msg_sem.at[0, peer],
            recv_sem=msg_sem.at[1, source],
            device_id={"pool": peer},
        )

    lane_id = lax.broadcasted_iota(jnp.int32, (qrows, hd), 1)
    diagonal = lane_id == lax.broadcasted_iota(jnp.int32, (qrows, hd), 0)
    sub16 = lax.broadcasted_iota(jnp.int32, (16, hd), 0)

    def last_chunk(i, carry):
        c = lax.rem(me // 4 + i, chunks)
        attend(b, c)
        for e in range(4):
            peer = c * 4 + e
            row = jnp.sum(jnp.where(diagonal, lse_v[peer], 0.0), axis=0, keepdims=True)
            high = row.astype(BF16).astype(F32)
            rest = row - high
            middle = rest.astype(BF16).astype(F32)
            low = rest - middle
            msg_v[peer, qrows:, :] = jnp.where(
                sub16 == 0,
                high,
                jnp.where(sub16 == 1, middle, jnp.where(sub16 == 2, low, 0.0)),
            ).astype(BF16)

            @pl.when(peer != me)
            def _():
                msg_copy(me, peer).start()

        return carry

    lax.fori_loop(0, chunks, last_chunk, 0)
    box_send(early, np_ - 1)

    for_peers(me, np_, lambda peer: msg_copy(peer, peer).wait_recv())
    outs = []
    lses = []
    row_lane = lax.rem(lax.broadcasted_iota(jnp.int32, (1, hd), 1), rows_dev)
    for i in range(PIECES):
        out = jnp.zeros((qrows, hd), F32)
        line = jnp.zeros((1, hd), F32)
        for r in range(rows_dev):
            source = hit_s[rowpref_s[me * rows_dev + r] * PIECES + i] // gb
            note = jnp.where(source == me, msg_v[me], back_v[source]).astype(F32)
            out = jnp.where(row_id == r, note[:qrows], out)
            text = jnp.sum(note[qrows:], axis=0, keepdims=True)
            line = jnp.where(row_lane == r, text, line)
        outs.append(out)
        lses.append(jnp.sum(jnp.where(diagonal, line, 0.0), axis=1, keepdims=True))
    res_peak = res_v[1]
    top = res_peak
    for lse in lses:
        top = jnp.maximum(top, lse)
    factor = jnp.exp(res_peak - top)
    numer = res_v[0] * factor
    denom = res_v[2] * factor
    for out, lse in zip(outs, lses):
        factor = jnp.exp(lse - top)
        numer = numer + out * factor
        denom = denom + factor
    attended = numer / denom
    att_ref[...] = jnp.concatenate(
        [attended[j * rows_dev : (j + 1) * rows_dev] for j in range(QUERY_GROUP)], axis=1
    ).astype(BF16)

    for_peers(me, np_, lambda peer: box_copy(0, peer).wait_recv())
    own_kv = kv_v[rank_sm[np_ - 1]]
    for j in range(gb):
        source = hit_s[me * gb + j] // gb
        cache_v[:, j * BLOCK : (j + 1) * BLOCK] = jnp.where(source == me, own_kv, inbox[source])
    out_copy = pltpu.make_async_copy(cache_v, cache_hbm, out_sem)
    out_copy.start()

    for rel in range(np_ - 1):
        box_copy(rel, me).wait_send()
    for_peers(me, np_, lambda peer: msg_copy(me, peer).wait_send())
    ring_drain(nb - 1)
    out_copy.wait()


def shards(
    pool_rows,
    hit_owner,
    norm_gain,
    kv_weight,
    queries,
    row_prefix,
    row_length,
    block_table,
    cache_keys,
    cache_values,
):
    np_ = lax.axis_size("pool")
    nh = lax.axis_size("head")
    gb = hit_owner.shape[0] // np_
    nb = gb // BATCH
    rows_dev = queries.shape[0]
    qrows = rows_dev * QUERY_GROUP
    features = pool_rows.shape[1]
    hd = HEAD_DIM
    cosine, sine = rotation_tables()
    smem = pl.BlockSpec(memory_space=pltpu.SMEM)
    vmem = pl.BlockSpec(memory_space=pltpu.VMEM)
    hbm = pl.BlockSpec(memory_space=pl.ANY)
    dma = pltpu.SemaphoreType.DMA
    half = BATCH // 2 * BLOCK
    cache, attended = pl.pallas_call(
        functools.partial(kernel, np_, nh, gb),
        out_shape=(
            jax.ShapeDtypeStruct((2 * hd, gb * BLOCK), BF16),
            jax.ShapeDtypeStruct(queries.shape, BF16),
        ),
        in_specs=[smem] * 4 + [vmem] * 4 + [hbm] * 4,
        out_specs=(hbm, vmem),
        scratch_shapes=[
            pltpu.SMEM((gb,), jnp.int32),
            pltpu.SMEM((np_,), jnp.int32),
            pltpu.VMEM((gb, BLOCK, features), BF16),
            pltpu.VMEM((nh, features, 2 * hd), BF16),
            pltpu.VMEM(cache_keys.shape[1:], BF16),
            pltpu.VMEM(cache_values.shape[1:], BF16),
            pltpu.VMEM((nb, 2, half, features), BF16),
            pltpu.VMEM((2, half, 2 * hd), F32),
            pltpu.VMEM((2, nb, nh, LANES, half // LANES, 2 * hd), BF16),
            pltpu.VMEM((nb // 2, 8, BLOCK), F32),
            pltpu.VMEM((nb // 2, nh, 8, BLOCK), F32),
            pltpu.VMEM((gb, 2 * hd, BLOCK), BF16),
            pltpu.VMEM((nb, 2 * hd, BATCH * BLOCK), BF16),
            pltpu.VMEM((np_ - 1, 2 * hd, BLOCK), BF16),
            pltpu.VMEM((np_, 2 * hd, BLOCK), BF16),
            pltpu.VMEM((2 * hd, gb * BLOCK), BF16),
            pltpu.VMEM((qrows, hd), BF16),
            pltpu.VMEM((np_, qrows, hd), BF16),
            pltpu.VMEM((np_, rows_dev, hd), jnp.int32),
            pltpu.VMEM((np_, qrows, hd), F32),
            pltpu.VMEM((np_, qrows + 16, hd), BF16),
            pltpu.VMEM((np_, qrows + 16, hd), BF16),
            pltpu.VMEM((3, qrows, hd), F32),
            dma,
            dma((nh,)),
            dma((2,)),
            dma((2, nb, LANES, 2)),
            dma((2, nb, nh - 1, LANES)),
            dma((2, nb // 2, nh)),
            dma((2, np_)),
            dma((2, np_)),
            dma((2, np_)),
            dma,
        ],
        compiler_params=pltpu.CompilerParams(
            collective_id=0, has_side_effects=True, vmem_limit_bytes=56 * 2**20
        ),
    )(
        hit_owner,
        row_prefix,
        row_length,
        block_table.T,
        norm_gain.reshape(1, features),
        jnp.asarray(cosine),
        jnp.asarray(sine),
        queries,
        pool_rows.reshape(gb, BLOCK, features),
        kv_weight,
        cache_keys[0],
        cache_values[0],
    )
    return cache[None], attended


def solution(mesh):
    return jax.shard_map(
        shards,
        mesh=mesh,
        in_specs=(
            P("pool", "head"),
            P(),
            P("head"),
            P("head", None),
            P("pool", "head"),
            P(),
            P("pool"),
            P("pool", None),
            P("head", "pool", None, None),
            P("head", "pool", None, None),
        ),
        out_specs=(P("head", None, "pool"), P("pool", "head")),
        check_vma=False,
    )
```

```python
import functools
import math

import jax
import jax.numpy as jnp
import numpy as np
from jax import lax
from jax.experimental import pallas as pl
from jax.experimental.pallas import tpu as pltpu
from jax.sharding import PartitionSpec as P

HEAD_DIM = 128
QUERY_GROUP = 8
BLOCK = 128
PIECES = 4
BATCH = 4
LANES = 2
F32 = jnp.float32
BF16 = jnp.bfloat16
NN = (((1,), (0,)), ((), ()))
NT = (((1,), (1,)), ((), ()))


def rotation_tables():
    half = HEAD_DIM // 2
    freqs = np.exp(np.arange(half) * (-2.0 / HEAD_DIM) * math.log(500000.0))
    positions = np.arange(PIECES * BLOCK).reshape(PIECES, 1, BLOCK)
    angles = positions * freqs[None, :, None]
    return np.cos(angles).astype(np.float32), np.sin(angles).astype(np.float32)


def offsets(np_):
    wide = 4 if np_ >= 32 else 2
    high = np_ // (2 * wide)

    def key(step):
        y, x, core = step
        far_y, far_x = min(y, high - y), min(x, wide - x)
        straight = far_y == 0 or far_x == 0
        return (-(far_y + far_x), not straight, core if far_y + far_x else -core, y, x)

    return wide, high, sorted(
        ((y, x, core) for y in range(high) for x in range(wide) for core in range(2)), key=key
    )


def kernel(
    np_,
    nh,
    gb,
    hit_s,
    rowpref_s,
    rowlen_s,
    table_s,
    gain_ref,
    cos_ref,
    sin_ref,
    query_ref,
    x_hbm,
    w_hbm,
    keys_hbm,
    vals_hbm,
    inbox,
    att_ref,
    hits_sm,
    rank_sm,
    x_v,
    w_v,
    keys_v,
    vals_v,
    xs_v,
    part_v,
    ring_v,
    ss_own,
    ss_v,
    kv_v,
    wide_v,
    outbox,
    own_q,
    q_v,
    pref_v,
    lse_v,
    msg_v,
    back_v,
    res_v,
    x_sem,
    w_sem,
    page_sem,
    ring_send,
    ring_recv,
    ss_sem,
    q_sem,
    box_sem,
    msg_sem,
    own_sem,
):
    me = lax.axis_index("pool")
    z = lax.axis_index("head")
    nb = gb // BATCH
    last = nh - 2
    steps = nh - 1
    dim = x_hbm.shape[2] * nh
    rows_dev = rowlen_s.shape[0]
    row_blocks = table_s.shape[0]
    qrows = rows_dev * QUERY_GROUP
    hd = HEAD_DIM
    scale = hd ** (-0.5)
    up = lax.rem(z + 1, nh)
    down = lax.rem(z + nh - 1, nh)
    half = BATCH // 2 * BLOCK
    sub8 = lax.broadcasted_iota(jnp.int32, (8, hd), 0)
    lane_rows = half // LANES

    wide_x, high_y, hops = offsets(np_)
    core = lax.rem(me, 2)
    at_x = lax.rem(lax.div(me, 2), wide_x)
    at_y = lax.div(me, 2 * wide_x)

    def dest(rel):
        y, x, c = hops[rel]
        return (lax.rem(at_y + y, high_y) * wide_x + lax.rem(at_x + x, wide_x)) * 2 + lax.rem(
            core + c, 2
        )

    def w_copy(h):
        return pltpu.make_async_copy(
            w_hbm.at[:, pl.ds(pl.multiple_of(h * 2 * hd, 2 * hd), 2 * hd)], w_v.at[h], w_sem.at[h]
        )

    x_copy = pltpu.make_async_copy(x_hbm, x_v, x_sem)
    for s in range(nh // 2):
        w_copy(lax.rem(z + nh - 1 - s, nh)).start()
        if s + 1 < nh - 1 - s:
            w_copy(lax.rem(z + 1 + s, nh)).start()
        if s == 0:
            x_copy.start()
    w_copy(z).start()
    key_copy = pltpu.make_async_copy(keys_hbm, keys_v, page_sem.at[0])
    val_copy = pltpu.make_async_copy(vals_hbm, vals_v, page_sem.at[1])
    key_copy.start()
    val_copy.start()

    query = query_ref[...].astype(F32)
    stacked = jnp.concatenate([query[:, j * hd : (j + 1) * hd] for j in range(QUERY_GROUP)], axis=0)
    own_q[...] = stacked.astype(BF16)
    q_v[me] = stacked.astype(BF16)

    barrier = pltpu.get_barrier_semaphore()

    def greet_pool(i, c):
        pl.semaphore_signal(barrier, inc=1, device_id={"pool": lax.rem(me + i, np_)})
        return c

    lax.fori_loop(1, np_, greet_pool, 0)

    def greet_head(i, c):
        pl.semaphore_signal(barrier, inc=1, device_id={"head": lax.rem(z + i, nh)})
        return c

    lax.fori_loop(1, nh, greet_head, 0)

    count = jnp.int32(0)
    found = [jnp.int32(0)] * gb
    for rel in range(np_):
        base = dest(rel) * gb
        hit = jnp.int32(-1)
        for t in range(gb):
            holder = hit_s[base + t]
            mine = jnp.logical_and(holder >= me * gb, holder < me * gb + gb)
            hit = jnp.where(mine, base + t, hit)
        present = hit >= 0
        rank_sm[rel] = jnp.minimum(count, gb - 1)
        for i in range(max(0, rel - (np_ - gb)), min(rel + 1, gb)):
            found[i] = jnp.where(jnp.logical_and(present, count == i), hit, found[i])
        count = count + present.astype(jnp.int32)
    for i in range(gb):
        hits_sm[i] = found[i]

    def q_copy(source, peer):
        return pltpu.make_async_remote_copy(
            src_ref=own_q,
            dst_ref=q_v.at[source],
            send_sem=q_sem.at[0, peer],
            recv_sem=q_sem.at[1, source],
            device_id={"pool": peer},
        )

    def for_peers(mine, n, act):
        def one(i, c):
            act(lax.rem(mine + i, n))
            return c

        lax.fori_loop(1, n, one, 0)

    def held(b, t):
        return x_v[hit_s[hits_sm[b * BATCH + t]] % gb].astype(F32)

    def scale_rows(b):
        for t in range(BATCH):
            xs_v[b, t // 2, (t % 2) * BLOCK : (t % 2 + 1) * BLOCK, :] = (
                held(b, t) * gain_ref[...]
            ).astype(BF16)

    def square_rows(b):
        for t in range(BATCH):
            block = held(b, t)
            square = block * block
            fold = square[:, :hd]
            for c in range(1, square.shape[1] // hd):
                fold = fold + square[:, c * hd : (c + 1) * hd]
            sums = lax.dot_general(
                jnp.ones((8, hd), F32),
                fold,
                NT,
                precision=lax.Precision.HIGHEST,
                preferred_element_type=F32,
            )
            ss_own[b // 2] = jnp.where(sub8 == b % 2 * BATCH + t, sums, ss_own[b // 2])

    def prepare(b):
        scale_rows(b)
        square_rows(b)

    def ss_copy(pair, source, peer):
        return pltpu.make_async_remote_copy(
            src_ref=ss_own.at[pair],
            dst_ref=ss_v.at[pair, source],
            send_sem=ss_sem.at[0, pair, peer],
            recv_sem=ss_sem.at[1, pair, source],
            device_id={"head": peer},
        )

    def ss_send(pair):
        for_peers(z, nh, lambda peer: ss_copy(pair, z, peer).start())

    def ring_copy(way, b, s, lane, parity):
        return pltpu.make_async_remote_copy(
            src_ref=ring_v.at[way, b, s, lane],
            dst_ref=ring_v.at[way, b, s + 1, lane],
            send_sem=ring_send.at[way, b, lane, parity],
            recv_sem=ring_recv.at[way, b, s, lane],
            device_id={"head": up if way == 0 else down},
        )

    def multiply(way, b, h):
        return lax.dot_general(xs_v[b, way], w_v[h], NN, preferred_element_type=F32)

    def finish(way, b):
        part_v[way] = multiply(way, b, z)
        for t in range(BATCH // 2):
            i = b * BATCH + way * (BATCH // 2) + t
            per = LANES // (BATCH // 2)
            for lane in range(t * per, (t + 1) * per):
                ring_copy(way, b, last, lane, 0).wait_recv()
            total = part_v[way, t * BLOCK : (t + 1) * BLOCK, :] + jnp.concatenate(
                [ring_v[way, b, last + 1, lane] for lane in range(t * per, (t + 1) * per)], axis=0
            ).astype(F32)
            tiles = ss_own[b // 2]
            for other in range(1, nh):
                tiles = tiles + ss_v[b // 2, lax.rem(z + other, nh)]
            row = b % 2 * BATCH + way * 2 + t
            squares = jnp.sum(jnp.where(sub8 == row, tiles, 0.0), axis=0, keepdims=True)
            normed = jnp.transpose(total) * lax.rsqrt(squares / dim + 1e-05)
            first = normed[: hd // 2]
            second = normed[hd // 2 : hd]
            piece = hits_sm[i] % PIECES
            cosine = cos_ref[piece]
            sine = sin_ref[piece]
            both = jnp.concatenate(
                [first * cosine - second * sine, second * cosine + first * sine, normed[hd:]],
                axis=0,
            ).astype(BF16)
            kv_v[i] = both
            place = way * (BATCH // 2) + t
            wide_v[b, :, place * BLOCK : (place + 1) * BLOCK] = both

    def box_copy(rel, source):
        return pltpu.make_async_remote_copy(
            src_ref=outbox.at[rel],
            dst_ref=inbox.at[source],
            send_sem=box_sem.at[0, rel],
            recv_sem=box_sem.at[1, source],
            device_id={"pool": dest(rel)},
        )

    def box_send(start, stop):
        for rel in range(start, stop):
            outbox[rel] = kv_v[rank_sm[rel]]
            box_copy(rel, me).start()

    def attend(b, c):
        wide = 4
        q = q_v[pl.ds(c * wide, wide)].reshape(wide * qrows, hd)
        rowpref = jnp.broadcast_to(
            pref_v[pl.ds(c * wide, wide)][:, None], (wide, QUERY_GROUP, rows_dev, hd)
        ).reshape(wide * qrows, hd)
        every = lax.dot_general(q, wide_v[b, :hd], NN, preferred_element_type=F32)
        masks = [rowpref == hits_sm[b * BATCH + t] // PIECES for t in range(BATCH)]
        scores = every[:, :BLOCK]
        for t in range(1, BATCH):
            scores = jnp.where(masks[t], every[:, t * BLOCK : (t + 1) * BLOCK], scores)
        scores = scores * scale
        peak = jnp.max(scores, axis=1, keepdims=True)
        weights = jnp.exp(scores - peak)
        mass = jnp.sum(weights, axis=1, keepdims=True)
        spread = jnp.concatenate(
            [jnp.where(masks[t], weights, 0.0).astype(BF16) for t in range(BATCH)], axis=1
        )
        total = lax.dot_general(spread, wide_v[b, hd:], NT, preferred_element_type=F32)
        hit = functools.reduce(jnp.logical_or, masks)
        out = total / mass
        lse = jnp.broadcast_to(peak + jnp.log(mass), (wide * qrows, hd))
        rows = pl.ds(c * wide, wide)
        old = msg_v[rows, :qrows, :].reshape(wide * qrows, hd).astype(F32)
        msg_v[rows, :qrows, :] = jnp.where(hit, out, old).astype(BF16).reshape(wide, qrows, hd)
        old = lse_v[rows].reshape(wide * qrows, hd)
        lse_v[rows] = jnp.where(hit, lse, old).reshape(wide, qrows, hd)

    row_id = lax.rem(lax.broadcasted_iota(jnp.int32, (qrows, hd), 0), rows_dev)

    def resident(r):
        q = own_q[...]
        pages = [table_s[i, r] for i in range(row_blocks)]
        scores = (
            jnp.concatenate(
                [
                    lax.dot_general(q, keys_v[page], NT, preferred_element_type=F32)
                    for page in pages
                ],
                axis=1,
            )
            * scale
        )
        token = lax.broadcasted_iota(jnp.int32, scores.shape, 1)
        valid = token < rowlen_s[r]
        peak = jnp.max(jnp.where(valid, scores, -jnp.inf), axis=1, keepdims=True)
        weights = jnp.where(valid, jnp.exp(scores - peak), 0.0)
        mass = jnp.sum(weights, axis=1, keepdims=True)
        rounded = weights.astype(BF16)
        total = jnp.zeros((qrows, hd), F32)
        for i, page in enumerate(pages):
            total = total + lax.dot_general(
                rounded[:, i * BLOCK : (i + 1) * BLOCK],
                vals_v[page],
                NN,
                preferred_element_type=F32,
            )
        mine = row_id == r
        res_v[0] = jnp.where(mine, total, res_v[0])
        res_v[1] = jnp.where(mine, peak, res_v[1])
        res_v[2] = jnp.where(mine, mass, res_v[2])

    chunks = np_ // 4

    def ring_step(b, s):
        heads = (lax.rem(z + 2 * nh - 1 - s, nh), lax.rem(z + 1 + s, nh))
        first = s == 0
        parity = s % 2
        for way in range(2):
            part_v[way] = multiply(way, b, heads[way])
        if b == 0 and s == 0:
            pl.semaphore_wait(barrier, np_ - 1 + nh - 1)
        for lane in range(LANES):
            rows = slice(lane * lane_rows, (lane + 1) * lane_rows)
            for way in range(2):
                if first:
                    ring_v[way, b, 0, lane] = part_v[way, rows, :].astype(BF16)
                else:
                    ring_copy(way, b, s - 1, lane, parity).wait_recv()
                    ring_v[way, b, s, lane] = (
                        ring_v[way, b, s, lane].astype(F32) + part_v[way, rows, :]
                    ).astype(BF16)

                    if s >= 2:
                        ring_copy(way, b, s, lane, parity).wait_send()

                ring_copy(way, b, s, lane, parity).start()

    def ring_drain(b):
        for way in range(2):
            for lane in range(LANES):
                for parity in range(2):
                    ring_copy(way, b, 0, lane, parity).wait_send()

    def attend_all(b, start, stop):
        def one(c, carry):
            attend(b, c)
            return carry

        lax.fori_loop(start, stop, one, 0)

    def resident_rows(start, stop):
        def one(r, carry):
            resident(r)
            return carry

        lax.fori_loop(start, stop, one, 0)

    def ss_wait(pair):
        for_peers(z, nh, lambda peer: ss_copy(pair, peer, peer).wait_recv())

    def start_queries():
        for_peers(me, np_, lambda peer: q_copy(me, peer).start())
        sub = lax.broadcasted_iota(jnp.int32, (rows_dev, hd), 0)

        def fill(i, c):
            tile = jnp.zeros((rows_dev, hd), jnp.int32)
            for r in range(rows_dev):
                tile = jnp.where(sub == r, rowpref_s[i * rows_dev + r], tile)
            pref_v[i] = tile
            return c

        lax.fori_loop(0, np_, fill, 0)

    def finish_both(b):
        if b % 2 == 0:
            ss_wait(b // 2)
        else:
            for_peers(z, nh, lambda peer: ss_copy(b // 2, z, peer).wait_send())
        if b > 0:
            ring_drain(b - 1)
        finish(0, b)
        box_send(b * BATCH, b * BATCH + BATCH // 2)
        finish(1, b)
        box_send(b * BATCH + BATCH // 2, min((b + 1) * BATCH, np_ - 1))

    begin = [(b // 2) * steps + (b % 2) * 2 for b in range(nb)]
    total_rounds = begin[-1] + steps
    work = {r: [] for r in range(total_rounds)}
    work[0] += [lambda: scale_rows(1), lambda: square_rows(0), lambda: square_rows(1)]
    work[2] += [start_queries]
    for b in range(1, nb):
        ready = begin[b] - 1
        if b > 1:
            work[ready].append(functools.partial(prepare, b))
        if b % 2 == 1:
            work[ready].append(functools.partial(ss_send, b // 2))
    free = [r for r in range(1, begin[0] + steps)]
    for i, r in enumerate(free):
        lo, hi = i * rows_dev // len(free), (i + 1) * rows_dev // len(free)
        if lo < hi:
            work[r].append(functools.partial(resident_rows, lo, hi))
    work[free[-1]].append(lambda: for_peers(me, np_, lambda peer: q_copy(peer, peer).wait_recv()))
    work[free[-1]].append(lambda: for_peers(me, np_, lambda peer: q_copy(me, peer).wait_send()))
    for b in range(nb - 1):
        done = min(begin[b] + steps, total_rounds - 2)
        after = [r for r in range(done + 1, min(done + 3, total_rounds))]
        work[done].append(functools.partial(finish_both, b))
        for i, r in enumerate(after):
            lo, hi = i * chunks // len(after), (i + 1) * chunks // len(after)
            work[r].append(functools.partial(attend_all, b, lo, hi))
    x_copy.wait()
    scale_rows(0)
    for r in range(total_rounds):
        if r < nh // 2:
            w_copy(lax.rem(z + nh - 1 - r, nh)).wait()
            if r + 1 < nh - 1 - r:
                w_copy(lax.rem(z + 1 + r, nh)).wait()
        if r == 1:
            key_copy.wait()
            val_copy.wait()
            w_copy(z).wait()
        for b in range(nb):
            if begin[b] <= r < begin[b] + steps:
                ring_step(b, r - begin[b])
        for task in work[r]:
            task()

    b = nb - 1
    finish_both(b)
    early = min((nb - 1) * BATCH + 6, np_ - 1)
    box_send(nb * BATCH, early)

    def msg_copy(source, peer):
        return pltpu.make_async_remote_copy(
            src_ref=msg_v.at[peer],
            dst_ref=back_v.at[source],
            send_sem=msg_sem.at[0, peer],
            recv_sem=msg_sem.at[1, source],
            device_id={"pool": peer},
        )

    lane_id = lax.broadcasted_iota(jnp.int32, (qrows, hd), 1)
    diagonal = lane_id == lax.broadcasted_iota(jnp.int32, (qrows, hd), 0)
    sub16 = lax.broadcasted_iota(jnp.int32, (16, hd), 0)

    def last_chunk(i, carry):
        c = lax.rem(me // 4 + i, chunks)
        attend(b, c)
        for e in range(4):
            peer = c * 4 + e
            row = jnp.sum(jnp.where(diagonal, lse_v[peer], 0.0), axis=0, keepdims=True)
            high = row.astype(BF16).astype(F32)
            rest = row - high
            middle = rest.astype(BF16).astype(F32)
            low = rest - middle
            msg_v[peer, qrows:, :] = jnp.where(
                sub16 == 0,
                high,
                jnp.where(sub16 == 1, middle, jnp.where(sub16 == 2, low, 0.0)),
            ).astype(BF16)

            @pl.when(peer != me)
            def _():
                msg_copy(me, peer).start()

        return carry

    lax.fori_loop(0, chunks, last_chunk, 0)
    box_send(early, np_ - 1)
    outbox[np_ - 1] = kv_v[rank_sm[np_ - 1]]
    own_copy = pltpu.make_async_copy(outbox.at[np_ - 1], inbox.at[me], own_sem)
    own_copy.start()

    for_peers(me, np_, lambda peer: msg_copy(peer, peer).wait_recv())
    outs = []
    lses = []
    row_lane = lax.rem(lax.broadcasted_iota(jnp.int32, (1, hd), 1), rows_dev)
    for i in range(PIECES):
        out = jnp.zeros((qrows, hd), F32)
        line = jnp.zeros((1, hd), F32)
        for r in range(rows_dev):
            source = hit_s[rowpref_s[me * rows_dev + r] * PIECES + i] // gb
            note = jnp.where(source == me, msg_v[me], back_v[source]).astype(F32)
            out = jnp.where(row_id == r, note[:qrows], out)
            text = jnp.sum(note[qrows:], axis=0, keepdims=True)
            line = jnp.where(row_lane == r, text, line)
        outs.append(out)
        lses.append(jnp.sum(jnp.where(diagonal, line, 0.0), axis=1, keepdims=True))
    res_peak = res_v[1]
    top = res_peak
    for lse in lses:
        top = jnp.maximum(top, lse)
    factor = jnp.exp(res_peak - top)
    numer = res_v[0] * factor
    denom = res_v[2] * factor
    for out, lse in zip(outs, lses):
        factor = jnp.exp(lse - top)
        numer = numer + out * factor
        denom = denom + factor
    attended = numer / denom
    att_ref[...] = jnp.concatenate(
        [attended[j * rows_dev : (j + 1) * rows_dev] for j in range(QUERY_GROUP)], axis=1
    ).astype(BF16)

    for_peers(me, np_, lambda peer: msg_copy(me, peer).wait_send())
    ring_drain(nb - 1)
    for rel in range(np_ - 1):
        box_copy(rel, me).wait_send()
    own_copy.wait()
    for_peers(me, np_, lambda peer: box_copy(0, peer).wait_recv())


def assemble(gb, hit_s, inbox, att_in, cache_hbm, att_out, cache_v, att_v, in_sems, out_sems):
    me = lax.axis_index("pool")
    arrive, leave = [], []
    for j in range(gb):
        source = lax.div(hit_s[me * gb + j], gb)
        arrive.append(pltpu.make_async_copy(inbox.at[source], cache_v.at[j], in_sems.at[j]))
        leave.append(
            pltpu.make_async_copy(
                cache_v.at[j], cache_hbm.at[:, j * BLOCK : (j + 1) * BLOCK], out_sems.at[j]
            )
        )
    arrive.append(pltpu.make_async_copy(att_in, att_v, in_sems.at[gb]))
    leave.append(pltpu.make_async_copy(att_v, att_out, out_sems.at[gb]))
    for copy in arrive:
        copy.start()
    for first, second in zip(arrive, leave):
        first.wait()
        second.start()
    for copy in leave:
        copy.wait()


def shards(
    pool_rows,
    hit_owner,
    norm_gain,
    kv_weight,
    queries,
    row_prefix,
    row_length,
    block_table,
    cache_keys,
    cache_values,
):
    np_ = lax.axis_size("pool")
    nh = lax.axis_size("head")
    gb = hit_owner.shape[0] // np_
    nb = gb // BATCH
    rows_dev = queries.shape[0]
    qrows = rows_dev * QUERY_GROUP
    features = pool_rows.shape[1]
    hd = HEAD_DIM
    cosine, sine = rotation_tables()
    smem = pl.BlockSpec(memory_space=pltpu.SMEM)
    vmem = pl.BlockSpec(memory_space=pltpu.VMEM)
    hbm = pl.BlockSpec(memory_space=pl.ANY)
    dma = pltpu.SemaphoreType.DMA
    half = BATCH // 2 * BLOCK
    inbox, attended = pl.pallas_call(
        functools.partial(kernel, np_, nh, gb),
        out_shape=(
            jax.ShapeDtypeStruct((np_, 2 * hd, BLOCK), BF16),
            jax.ShapeDtypeStruct(queries.shape, BF16),
        ),
        in_specs=[smem] * 4 + [vmem] * 4 + [hbm] * 4,
        out_specs=(hbm, vmem),
        scratch_shapes=[
            pltpu.SMEM((gb,), jnp.int32),
            pltpu.SMEM((np_,), jnp.int32),
            pltpu.VMEM((gb, BLOCK, features), BF16),
            pltpu.VMEM((nh, features, 2 * hd), BF16),
            pltpu.VMEM(cache_keys.shape[1:], BF16),
            pltpu.VMEM(cache_values.shape[1:], BF16),
            pltpu.VMEM((nb, 2, half, features), BF16),
            pltpu.VMEM((2, half, 2 * hd), F32),
            pltpu.VMEM((2, nb, nh, LANES, half // LANES, 2 * hd), BF16),
            pltpu.VMEM((nb // 2, 8, BLOCK), F32),
            pltpu.VMEM((nb // 2, nh, 8, BLOCK), F32),
            pltpu.VMEM((gb, 2 * hd, BLOCK), BF16),
            pltpu.VMEM((nb, 2 * hd, BATCH * BLOCK), BF16),
            pltpu.VMEM((np_, 2 * hd, BLOCK), BF16),
            pltpu.VMEM((qrows, hd), BF16),
            pltpu.VMEM((np_, qrows, hd), BF16),
            pltpu.VMEM((np_, rows_dev, hd), jnp.int32),
            pltpu.VMEM((np_, qrows, hd), F32),
            pltpu.VMEM((np_, qrows + 16, hd), BF16),
            pltpu.VMEM((np_, qrows + 16, hd), BF16),
            pltpu.VMEM((3, qrows, hd), F32),
            dma,
            dma((nh,)),
            dma((2,)),
            dma((2, nb, LANES, 2)),
            dma((2, nb, nh - 1, LANES)),
            dma((2, nb // 2, nh)),
            dma((2, np_)),
            dma((2, np_)),
            dma((2, np_)),
            dma,
        ],
        compiler_params=pltpu.CompilerParams(
            collective_id=0, has_side_effects=True, vmem_limit_bytes=56 * 2**20
        ),
    )(
        hit_owner,
        row_prefix,
        row_length,
        block_table.T,
        norm_gain.reshape(1, features),
        jnp.asarray(cosine),
        jnp.asarray(sine),
        queries,
        pool_rows.reshape(gb, BLOCK, features),
        kv_weight,
        cache_keys[0],
        cache_values[0],
    )
    cache, attended = pl.pallas_call(
        functools.partial(assemble, gb),
        out_shape=(
            jax.ShapeDtypeStruct((2 * hd, gb * BLOCK), BF16),
            jax.ShapeDtypeStruct(queries.shape, BF16),
        ),
        in_specs=[smem, hbm, hbm],
        out_specs=(hbm, hbm),
        scratch_shapes=[
            pltpu.VMEM((gb, 2 * hd, BLOCK), BF16),
            pltpu.VMEM(queries.shape, BF16),
            dma((gb + 1,)),
            dma((gb + 1,)),
        ],
        compiler_params=pltpu.CompilerParams(vmem_limit_bytes=60 * 2**20),
    )(hit_owner, inbox, attended)
    return cache[None], attended


def solution(mesh):
    return jax.shard_map(
        shards,
        mesh=mesh,
        in_specs=(
            P("pool", "head"),
            P(),
            P("head"),
            P("head", None),
            P("pool", "head"),
            P(),
            P("pool"),
            P("pool", None),
            P("head", "pool", None, None),
            P("head", "pool", None, None),
        ),
        out_specs=(P("head", None, "pool"), P("pool", "head")),
        check_vma=False,
    )
```

```python
import functools
import math

import jax
import jax.numpy as jnp
import numpy as np
from jax import lax
from jax.experimental import pallas as pl
from jax.experimental.pallas import tpu as pltpu
from jax.sharding import PartitionSpec as P

HEAD_DIM = 128
QUERY_GROUP = 8
BLOCK = 128
PIECES = 4
BATCH = 4
LANES = 2
F32 = jnp.float32
BF16 = jnp.bfloat16
NN = (((1,), (0,)), ((), ()))
NT = (((1,), (1,)), ((), ()))


def rotation_tables():
    half = HEAD_DIM // 2
    freqs = np.exp(np.arange(half) * (-2.0 / HEAD_DIM) * math.log(500000.0))
    positions = np.arange(PIECES * BLOCK).reshape(PIECES, 1, BLOCK)
    angles = positions * freqs[None, :, None]
    return np.cos(angles).astype(np.float32), np.sin(angles).astype(np.float32)


def offsets(np_):
    wide = 4 if np_ >= 32 else 2
    high = np_ // (2 * wide)

    def key(step):
        y, x, core = step
        far_y, far_x = min(y, high - y), min(x, wide - x)
        straight = far_y == 0 or far_x == 0
        return (-(far_y + far_x), not straight, core if far_y + far_x else -core, y, x)

    return wide, high, sorted(
        ((y, x, core) for y in range(high) for x in range(wide) for core in range(2)), key=key
    )


def kernel(
    np_,
    nh,
    gb,
    hit_s,
    rowpref_s,
    rowlen_s,
    table_s,
    gain_ref,
    cos_ref,
    sin_ref,
    query_ref,
    x_hbm,
    w_hbm,
    keys_hbm,
    vals_hbm,
    inbox,
    att_ref,
    hits_sm,
    rank_sm,
    x_v,
    w_v,
    keys_v,
    vals_v,
    xs_v,
    part_v,
    ring_v,
    ss_own,
    ss_v,
    kv_v,
    wide_v,
    outbox,
    own_q,
    q_v,
    pref_v,
    lse_v,
    msg_v,
    back_v,
    note_v,
    told_v,
    res_v,
    x_sem,
    w_sem,
    page_sem,
    ring_send,
    ring_recv,
    ss_sem,
    q_sem,
    box_sem,
    msg_sem,
    note_sem,
    own_sem,
):
    me = lax.axis_index("pool")
    z = lax.axis_index("head")
    nb = gb // BATCH
    last = nh - 2
    steps = nh - 1
    dim = x_hbm.shape[2] * nh
    rows_dev = rowlen_s.shape[0]
    row_blocks = table_s.shape[0]
    qrows = rows_dev * QUERY_GROUP
    hd = HEAD_DIM
    scale = hd ** (-0.5)
    up = lax.rem(z + 1, nh)
    down = lax.rem(z + nh - 1, nh)
    half = BATCH // 2 * BLOCK
    sub8 = lax.broadcasted_iota(jnp.int32, (8, hd), 0)
    lane_rows = half // LANES

    wide_x, high_y, hops = offsets(np_)
    core = lax.rem(me, 2)
    at_x = lax.rem(lax.div(me, 2), wide_x)
    at_y = lax.div(me, 2 * wide_x)

    def dest(rel):
        y, x, c = hops[rel]
        return (lax.rem(at_y + y, high_y) * wide_x + lax.rem(at_x + x, wide_x)) * 2 + lax.rem(
            core + c, 2
        )

    def w_copy(h):
        return pltpu.make_async_copy(
            w_hbm.at[:, pl.ds(pl.multiple_of(h * 2 * hd, 2 * hd), 2 * hd)], w_v.at[h], w_sem.at[h]
        )

    x_copy = pltpu.make_async_copy(x_hbm, x_v, x_sem)
    for s in range(nh // 2):
        w_copy(lax.rem(z + nh - 1 - s, nh)).start()
        if s + 1 < nh - 1 - s:
            w_copy(lax.rem(z + 1 + s, nh)).start()
        if s == 0:
            x_copy.start()
    w_copy(z).start()
    key_copy = pltpu.make_async_copy(keys_hbm, keys_v, page_sem.at[0])
    val_copy = pltpu.make_async_copy(vals_hbm, vals_v, page_sem.at[1])
    key_copy.start()
    val_copy.start()

    query = query_ref[...].astype(F32)
    stacked = jnp.concatenate([query[:, j * hd : (j + 1) * hd] for j in range(QUERY_GROUP)], axis=0)
    own_q[...] = stacked.astype(BF16)
    q_v[me] = stacked.astype(BF16)

    barrier = pltpu.get_barrier_semaphore()

    def greet_pool(i, c):
        pl.semaphore_signal(barrier, inc=1, device_id={"pool": lax.rem(me + i, np_)})
        return c

    lax.fori_loop(1, np_, greet_pool, 0)

    def greet_head(i, c):
        pl.semaphore_signal(barrier, inc=1, device_id={"head": lax.rem(z + i, nh)})
        return c

    lax.fori_loop(1, nh, greet_head, 0)

    count = jnp.int32(0)
    found = [jnp.int32(0)] * gb
    for rel in range(np_):
        base = dest(rel) * gb
        hit = jnp.int32(-1)
        for t in range(gb):
            holder = hit_s[base + t]
            mine = jnp.logical_and(holder >= me * gb, holder < me * gb + gb)
            hit = jnp.where(mine, base + t, hit)
        present = hit >= 0
        rank_sm[rel] = jnp.minimum(count, gb - 1)
        for i in range(max(0, rel - (np_ - gb)), min(rel + 1, gb)):
            found[i] = jnp.where(jnp.logical_and(present, count == i), hit, found[i])
        count = count + present.astype(jnp.int32)
    for i in range(gb):
        hits_sm[i] = found[i]

    def q_copy(source, peer):
        return pltpu.make_async_remote_copy(
            src_ref=own_q,
            dst_ref=q_v.at[source],
            send_sem=q_sem.at[0, peer],
            recv_sem=q_sem.at[1, source],
            device_id={"pool": peer},
        )

    def for_peers(mine, n, act):
        def one(i, c):
            act(lax.rem(mine + i, n))
            return c

        lax.fori_loop(1, n, one, 0)

    def held(b, t):
        return x_v[hit_s[hits_sm[b * BATCH + t]] % gb].astype(F32)

    def scale_rows(b):
        for t in range(BATCH):
            xs_v[b, t // 2, (t % 2) * BLOCK : (t % 2 + 1) * BLOCK, :] = (
                held(b, t) * gain_ref[...]
            ).astype(BF16)

    def square_rows(b):
        for t in range(BATCH):
            block = held(b, t)
            square = block * block
            fold = square[:, :hd]
            for c in range(1, square.shape[1] // hd):
                fold = fold + square[:, c * hd : (c + 1) * hd]
            sums = lax.dot_general(
                jnp.ones((8, hd), F32),
                fold,
                NT,
                precision=lax.Precision.HIGHEST,
                preferred_element_type=F32,
            )
            ss_own[b // 2] = jnp.where(sub8 == b % 2 * BATCH + t, sums, ss_own[b // 2])

    def prepare(b):
        scale_rows(b)
        square_rows(b)

    def ss_copy(pair, source, peer):
        return pltpu.make_async_remote_copy(
            src_ref=ss_own.at[pair],
            dst_ref=ss_v.at[pair, source],
            send_sem=ss_sem.at[0, pair, peer],
            recv_sem=ss_sem.at[1, pair, source],
            device_id={"head": peer},
        )

    def ss_send(pair):
        for_peers(z, nh, lambda peer: ss_copy(pair, z, peer).start())

    def ring_copy(way, b, s, lane, parity):
        return pltpu.make_async_remote_copy(
            src_ref=ring_v.at[way, b, s, lane],
            dst_ref=ring_v.at[way, b, s + 1, lane],
            send_sem=ring_send.at[way, b, lane, parity],
            recv_sem=ring_recv.at[way, b, s, lane],
            device_id={"head": up if way == 0 else down},
        )

    def multiply(way, b, h):
        return lax.dot_general(xs_v[b, way], w_v[h], NN, preferred_element_type=F32)

    def finish(way, b):
        part_v[way] = multiply(way, b, z)
        for t in range(BATCH // 2):
            i = b * BATCH + way * (BATCH // 2) + t
            per = LANES // (BATCH // 2)
            for lane in range(t * per, (t + 1) * per):
                ring_copy(way, b, last, lane, 0).wait_recv()
            total = part_v[way, t * BLOCK : (t + 1) * BLOCK, :] + jnp.concatenate(
                [ring_v[way, b, last + 1, lane] for lane in range(t * per, (t + 1) * per)], axis=0
            ).astype(F32)
            tiles = ss_own[b // 2]
            for other in range(1, nh):
                tiles = tiles + ss_v[b // 2, lax.rem(z + other, nh)]
            row = b % 2 * BATCH + way * 2 + t
            squares = jnp.sum(jnp.where(sub8 == row, tiles, 0.0), axis=0, keepdims=True)
            normed = jnp.transpose(total) * lax.rsqrt(squares / dim + 1e-05)
            first = normed[: hd // 2]
            second = normed[hd // 2 : hd]
            piece = hits_sm[i] % PIECES
            cosine = cos_ref[piece]
            sine = sin_ref[piece]
            both = jnp.concatenate(
                [first * cosine - second * sine, second * cosine + first * sine, normed[hd:]],
                axis=0,
            ).astype(BF16)
            kv_v[i] = both
            place = way * (BATCH // 2) + t
            wide_v[b, :, place * BLOCK : (place + 1) * BLOCK] = both

    def box_copy(rel, source):
        return pltpu.make_async_remote_copy(
            src_ref=outbox.at[rel],
            dst_ref=inbox.at[source],
            send_sem=box_sem.at[0, rel],
            recv_sem=box_sem.at[1, source],
            device_id={"pool": dest(rel)},
        )

    def box_send(start, stop):
        for rel in range(start, stop):
            outbox[rel] = kv_v[rank_sm[rel]]
            box_copy(rel, me).start()

    def attend(b, c):
        wide = 4
        q = q_v[pl.ds(c * wide, wide)].reshape(wide * qrows, hd)
        rowpref = jnp.broadcast_to(
            pref_v[pl.ds(c * wide, wide)][:, None], (wide, QUERY_GROUP, rows_dev, hd)
        ).reshape(wide * qrows, hd)
        every = lax.dot_general(q, wide_v[b, :hd], NN, preferred_element_type=F32)
        masks = [rowpref == hits_sm[b * BATCH + t] // PIECES for t in range(BATCH)]
        scores = every[:, :BLOCK]
        for t in range(1, BATCH):
            scores = jnp.where(masks[t], every[:, t * BLOCK : (t + 1) * BLOCK], scores)
        scores = scores * scale
        peak = jnp.max(scores, axis=1, keepdims=True)
        weights = jnp.exp(scores - peak)
        mass = jnp.sum(weights, axis=1, keepdims=True)
        spread = jnp.concatenate(
            [jnp.where(masks[t], weights, 0.0).astype(BF16) for t in range(BATCH)], axis=1
        )
        total = lax.dot_general(spread, wide_v[b, hd:], NT, preferred_element_type=F32)
        hit = functools.reduce(jnp.logical_or, masks)
        out = total / mass
        lse = jnp.broadcast_to(peak + jnp.log(mass), (wide * qrows, hd))
        rows = pl.ds(c * wide, wide)
        old = msg_v[rows, :qrows, :].reshape(wide * qrows, hd).astype(F32)
        msg_v[rows, :qrows, :] = jnp.where(hit, out, old).astype(BF16).reshape(wide, qrows, hd)
        old = lse_v[rows].reshape(wide * qrows, hd)
        lse_v[rows] = jnp.where(hit, lse, old).reshape(wide, qrows, hd)

    row_id = lax.rem(lax.broadcasted_iota(jnp.int32, (qrows, hd), 0), rows_dev)

    def resident(r):
        q = own_q[...]
        pages = [table_s[i, r] for i in range(row_blocks)]
        scores = (
            jnp.concatenate(
                [
                    lax.dot_general(q, keys_v[page], NT, preferred_element_type=F32)
                    for page in pages
                ],
                axis=1,
            )
            * scale
        )
        token = lax.broadcasted_iota(jnp.int32, scores.shape, 1)
        valid = token < rowlen_s[r]
        peak = jnp.max(jnp.where(valid, scores, -jnp.inf), axis=1, keepdims=True)
        weights = jnp.where(valid, jnp.exp(scores - peak), 0.0)
        mass = jnp.sum(weights, axis=1, keepdims=True)
        rounded = weights.astype(BF16)
        total = jnp.zeros((qrows, hd), F32)
        for i, page in enumerate(pages):
            total = total + lax.dot_general(
                rounded[:, i * BLOCK : (i + 1) * BLOCK],
                vals_v[page],
                NN,
                preferred_element_type=F32,
            )
        mine = row_id == r
        res_v[0] = jnp.where(mine, total, res_v[0])
        res_v[1] = jnp.where(mine, peak, res_v[1])
        res_v[2] = jnp.where(mine, mass, res_v[2])

    chunks = np_ // 4

    def ring_step(b, s):
        heads = (lax.rem(z + 2 * nh - 1 - s, nh), lax.rem(z + 1 + s, nh))
        first = s == 0
        parity = s % 2
        for way in range(2):
            part_v[way] = multiply(way, b, heads[way])
        if b == 0 and s == 0:
            pl.semaphore_wait(barrier, np_ - 1 + nh - 1)
        for lane in range(LANES):
            rows = slice(lane * lane_rows, (lane + 1) * lane_rows)
            for way in range(2):
                if first:
                    ring_v[way, b, 0, lane] = part_v[way, rows, :].astype(BF16)
                else:
                    ring_copy(way, b, s - 1, lane, parity).wait_recv()
                    ring_v[way, b, s, lane] = (
                        ring_v[way, b, s, lane].astype(F32) + part_v[way, rows, :]
                    ).astype(BF16)

                    if s >= 2:
                        ring_copy(way, b, s, lane, parity).wait_send()

                ring_copy(way, b, s, lane, parity).start()

    def ring_drain(b):
        for way in range(2):
            for lane in range(LANES):
                for parity in range(2):
                    ring_copy(way, b, 0, lane, parity).wait_send()

    def attend_all(b, start, stop):
        def one(c, carry):
            attend(b, c)
            return carry

        lax.fori_loop(start, stop, one, 0)

    def resident_rows(start, stop):
        def one(r, carry):
            resident(r)
            return carry

        lax.fori_loop(start, stop, one, 0)

    def ss_wait(pair):
        for_peers(z, nh, lambda peer: ss_copy(pair, peer, peer).wait_recv())

    def start_queries():
        for_peers(me, np_, lambda peer: q_copy(me, peer).start())
        sub = lax.broadcasted_iota(jnp.int32, (rows_dev, hd), 0)

        def fill(i, c):
            tile = jnp.zeros((rows_dev, hd), jnp.int32)
            for r in range(rows_dev):
                tile = jnp.where(sub == r, rowpref_s[i * rows_dev + r], tile)
            pref_v[i] = tile
            return c

        lax.fori_loop(0, np_, fill, 0)

    def finish_both(b):
        if b % 2 == 0:
            ss_wait(b // 2)
        else:
            for_peers(z, nh, lambda peer: ss_copy(b // 2, z, peer).wait_send())
        if b > 0:
            ring_drain(b - 1)
        finish(0, b)
        box_send(b * BATCH, b * BATCH + BATCH // 2)
        finish(1, b)
        box_send(b * BATCH + BATCH // 2, min((b + 1) * BATCH, np_ - 1))

    begin = [(b // 2) * steps + (b % 2) * 2 for b in range(nb)]
    total_rounds = begin[-1] + steps
    work = {r: [] for r in range(total_rounds)}
    work[0] += [lambda: scale_rows(1), lambda: square_rows(0), lambda: square_rows(1)]
    work[2] += [start_queries]
    for b in range(1, nb):
        ready = begin[b] - 1
        if b > 1:
            work[ready].append(functools.partial(prepare, b))
        if b % 2 == 1:
            work[ready].append(functools.partial(ss_send, b // 2))
    free = [r for r in range(1, begin[0] + steps)]
    for i, r in enumerate(free):
        lo, hi = i * rows_dev // len(free), (i + 1) * rows_dev // len(free)
        if lo < hi:
            work[r].append(functools.partial(resident_rows, lo, hi))
    work[free[-1]].append(lambda: for_peers(me, np_, lambda peer: q_copy(peer, peer).wait_recv()))
    work[free[-1]].append(lambda: for_peers(me, np_, lambda peer: q_copy(me, peer).wait_send()))
    for b in range(nb - 1):
        done = min(begin[b] + steps, total_rounds - 2)
        after = [r for r in range(done + 1, min(done + 3, total_rounds))]
        work[done].append(functools.partial(finish_both, b))
        for i, r in enumerate(after):
            lo, hi = i * chunks // len(after), (i + 1) * chunks // len(after)
            work[r].append(functools.partial(attend_all, b, lo, hi))
    x_copy.wait()
    scale_rows(0)
    for r in range(total_rounds):
        if r < nh // 2:
            w_copy(lax.rem(z + nh - 1 - r, nh)).wait()
            if r + 1 < nh - 1 - r:
                w_copy(lax.rem(z + 1 + r, nh)).wait()
        if r == 1:
            key_copy.wait()
            val_copy.wait()
            w_copy(z).wait()
        for b in range(nb):
            if begin[b] <= r < begin[b] + steps:
                ring_step(b, r - begin[b])
        for task in work[r]:
            task()

    b = nb - 1
    finish_both(b)
    early = min((nb - 1) * BATCH + 6, np_ - 1)
    box_send(nb * BATCH, early)

    def msg_copy(source, peer):
        return pltpu.make_async_remote_copy(
            src_ref=msg_v.at[peer],
            dst_ref=back_v.at[source],
            send_sem=msg_sem.at[0, peer],
            recv_sem=msg_sem.at[1, source],
            device_id={"pool": peer},
        )

    lane_id = lax.broadcasted_iota(jnp.int32, (qrows, hd), 1)
    diagonal = lane_id == lax.broadcasted_iota(jnp.int32, (qrows, hd), 0)

    def note_copy(source, peer):
        return pltpu.make_async_remote_copy(
            src_ref=note_v.at[peer],
            dst_ref=told_v.at[source],
            send_sem=note_sem.at[0, peer],
            recv_sem=note_sem.at[1, source],
            device_id={"pool": peer},
        )

    def last_chunk(i, carry):
        c = lax.rem(me // 4 + i, chunks)
        attend(b, c)
        for e in range(4):
            peer = c * 4 + e
            row = jnp.sum(jnp.where(diagonal, lse_v[peer], 0.0), axis=0, keepdims=True)
            note_v[peer] = row

            @pl.when(peer != me)
            def _():
                note_copy(me, peer).start()
                msg_copy(me, peer).start()

        return carry

    lax.fori_loop(0, chunks, last_chunk, 0)
    box_send(early, np_ - 1)
    outbox[np_ - 1] = kv_v[rank_sm[np_ - 1]]
    own_copy = pltpu.make_async_copy(outbox.at[np_ - 1], inbox.at[me], own_sem)
    own_copy.start()

    for_peers(me, np_, lambda peer: msg_copy(peer, peer).wait_recv())
    for_peers(me, np_, lambda peer: note_copy(peer, peer).wait_recv())
    outs = []
    lses = []
    row_lane = lax.rem(lax.broadcasted_iota(jnp.int32, (1, hd), 1), rows_dev)
    for i in range(PIECES):
        out = jnp.zeros((qrows, hd), F32)
        line = jnp.zeros((1, hd), F32)
        for r in range(rows_dev):
            source = hit_s[rowpref_s[me * rows_dev + r] * PIECES + i] // gb
            note = jnp.where(source == me, msg_v[me], back_v[source]).astype(F32)
            out = jnp.where(row_id == r, note, out)
            text = jnp.where(source == me, note_v[me], told_v[source])
            line = jnp.where(row_lane == r, text, line)
        outs.append(out)
        lses.append(jnp.sum(jnp.where(diagonal, line, 0.0), axis=1, keepdims=True))
    res_peak = res_v[1]
    top = res_peak
    for lse in lses:
        top = jnp.maximum(top, lse)
    factor = jnp.exp(res_peak - top)
    numer = res_v[0] * factor
    denom = res_v[2] * factor
    for out, lse in zip(outs, lses):
        factor = jnp.exp(lse - top)
        numer = numer + out * factor
        denom = denom + factor
    attended = numer / denom
    att_ref[...] = jnp.concatenate(
        [attended[j * rows_dev : (j + 1) * rows_dev] for j in range(QUERY_GROUP)], axis=1
    ).astype(BF16)

    for_peers(me, np_, lambda peer: msg_copy(me, peer).wait_send())
    for_peers(me, np_, lambda peer: note_copy(me, peer).wait_send())
    ring_drain(nb - 1)
    for rel in range(np_ - 1):
        box_copy(rel, me).wait_send()
    own_copy.wait()
    for_peers(me, np_, lambda peer: box_copy(0, peer).wait_recv())


def assemble(gb, hit_s, inbox, att_in, cache_hbm, att_out, cache_v, att_v, in_sems, out_sems):
    me = lax.axis_index("pool")
    arrive, leave = [], []
    for j in range(gb):
        source = lax.div(hit_s[me * gb + j], gb)
        arrive.append(pltpu.make_async_copy(inbox.at[source], cache_v.at[j], in_sems.at[j]))
        leave.append(
            pltpu.make_async_copy(
                cache_v.at[j], cache_hbm.at[:, j * BLOCK : (j + 1) * BLOCK], out_sems.at[j]
            )
        )
    arrive.append(pltpu.make_async_copy(att_in, att_v, in_sems.at[gb]))
    leave.append(pltpu.make_async_copy(att_v, att_out, out_sems.at[gb]))
    for copy in arrive:
        copy.start()
    for first, second in zip(arrive, leave):
        first.wait()
        second.start()
    for copy in leave:
        copy.wait()


def shards(
    pool_rows,
    hit_owner,
    norm_gain,
    kv_weight,
    queries,
    row_prefix,
    row_length,
    block_table,
    cache_keys,
    cache_values,
):
    np_ = lax.axis_size("pool")
    nh = lax.axis_size("head")
    gb = hit_owner.shape[0] // np_
    nb = gb // BATCH
    rows_dev = queries.shape[0]
    qrows = rows_dev * QUERY_GROUP
    features = pool_rows.shape[1]
    hd = HEAD_DIM
    cosine, sine = rotation_tables()
    smem = pl.BlockSpec(memory_space=pltpu.SMEM)
    vmem = pl.BlockSpec(memory_space=pltpu.VMEM)
    hbm = pl.BlockSpec(memory_space=pl.ANY)
    dma = pltpu.SemaphoreType.DMA
    half = BATCH // 2 * BLOCK
    inbox, attended = pl.pallas_call(
        functools.partial(kernel, np_, nh, gb),
        out_shape=(
            jax.ShapeDtypeStruct((np_, 2 * hd, BLOCK), BF16),
            jax.ShapeDtypeStruct(queries.shape, BF16),
        ),
        in_specs=[smem] * 4 + [vmem] * 4 + [hbm] * 4,
        out_specs=(hbm, vmem),
        scratch_shapes=[
            pltpu.SMEM((gb,), jnp.int32),
            pltpu.SMEM((np_,), jnp.int32),
            pltpu.VMEM((gb, BLOCK, features), BF16),
            pltpu.VMEM((nh, features, 2 * hd), BF16),
            pltpu.VMEM(cache_keys.shape[1:], BF16),
            pltpu.VMEM(cache_values.shape[1:], BF16),
            pltpu.VMEM((nb, 2, half, features), BF16),
            pltpu.VMEM((2, half, 2 * hd), F32),
            pltpu.VMEM((2, nb, nh, LANES, half // LANES, 2 * hd), BF16),
            pltpu.VMEM((nb // 2, 8, BLOCK), F32),
            pltpu.VMEM((nb // 2, nh, 8, BLOCK), F32),
            pltpu.VMEM((gb, 2 * hd, BLOCK), BF16),
            pltpu.VMEM((nb, 2 * hd, BATCH * BLOCK), BF16),
            pltpu.VMEM((np_, 2 * hd, BLOCK), BF16),
            pltpu.VMEM((qrows, hd), BF16),
            pltpu.VMEM((np_, qrows, hd), BF16),
            pltpu.VMEM((np_, rows_dev, hd), jnp.int32),
            pltpu.VMEM((np_, qrows, hd), F32),
            pltpu.VMEM((np_, qrows, hd), BF16),
            pltpu.VMEM((np_, qrows, hd), BF16),
            pltpu.VMEM((np_, 1, hd), F32),
            pltpu.VMEM((np_, 1, hd), F32),
            pltpu.VMEM((3, qrows, hd), F32),
            dma,
            dma((nh,)),
            dma((2,)),
            dma((2, nb, LANES, 2)),
            dma((2, nb, nh - 1, LANES)),
            dma((2, nb // 2, nh)),
            dma((2, np_)),
            dma((2, np_)),
            dma((2, np_)),
            dma((2, np_)),
            dma,
        ],
        compiler_params=pltpu.CompilerParams(
            collective_id=0, has_side_effects=True, vmem_limit_bytes=56 * 2**20
        ),
    )(
        hit_owner,
        row_prefix,
        row_length,
        block_table.T,
        norm_gain.reshape(1, features),
        jnp.asarray(cosine),
        jnp.asarray(sine),
        queries,
        pool_rows.reshape(gb, BLOCK, features),
        kv_weight,
        cache_keys[0],
        cache_values[0],
    )
    cache, attended = pl.pallas_call(
        functools.partial(assemble, gb),
        out_shape=(
            jax.ShapeDtypeStruct((2 * hd, gb * BLOCK), BF16),
            jax.ShapeDtypeStruct(queries.shape, BF16),
        ),
        in_specs=[smem, hbm, hbm],
        out_specs=(hbm, hbm),
        scratch_shapes=[
            pltpu.VMEM((gb, 2 * hd, BLOCK), BF16),
            pltpu.VMEM(queries.shape, BF16),
            dma((gb + 1,)),
            dma((gb + 1,)),
        ],
        compiler_params=pltpu.CompilerParams(vmem_limit_bytes=60 * 2**20),
    )(hit_owner, inbox, attended)
    return cache[None], attended


def solution(mesh):
    return jax.shard_map(
        shards,
        mesh=mesh,
        in_specs=(
            P("pool", "head"),
            P(),
            P("head"),
            P("head", None),
            P("pool", "head"),
            P(),
            P("pool"),
            P("pool", None),
            P("head", "pool", None, None),
            P("head", "pool", None, None),
        ),
        out_specs=(P("head", None, "pool"), P("pool", "head")),
        check_vma=False,
    )
```
